256 devices in a mesh: seq: 32 (over y_hi, z, core), chan: 8 (over y_lo, x).
Axes of the slice: x: 4, y: 4 (y_hi: 2, y_lo: 2; y = y_hi * 2 + y_lo), z: 8, core: 2. Of those that a mesh axis runs over, the one named last changes fastest.
Arguments:
- proj: bfloat16 [3, 16384, 8192], P(None, 'seq', 'chan'), may hold values from -64 to 64
- short_weight: float32 [3, 7, 8192], P(None, None, 'chan'), may hold values from -40 to 40
- spectrum: bfloat16 [2, 64, 512, 8192], P(None, 'seq', None, 'chan'), as said below
- skip: float32 [8192], P('chan'), may hold values from 0.3 to 1.5
- gain: float32 [8192], P('chan'), may hold values from 0.5 to 1.5
Outputs:
- mixer_out: bfloat16 [32, 2, 256, 8192], P('seq', None, None, 'chan')
The draws below stay inside these ranges and needn't reach their ends.
Inputs may be any that keep to these rules, and one draw needn't show every extreme that they name: `spectrum`: the transform of a real causal filter per channel whose values at lags 16384 and beyond are zero.
All inputs are finite; a program needn't handle non-finite values.
Results may differ from the reference program's by a relative error of at most 0.0065.
Values may be sent and summed in bfloat16 or wider, within the bound.
A program may use at most 128 MiB of HBM per device.

```python
import math
import jax
import jax.numpy as jnp
from jax import lax

D = 8192
ROWS = 512
TAPS = 7
SHARDS = 32
LENGTH = 16384
SPAN = 32768


def draw_proj(key, part):
    key = jax.random.fold_in(key, 11)
    base_key, row_key = jax.random.split(key)
    base = jnp.clip(jax.random.normal(base_key, (3, LENGTH, D), jnp.float32), -4.0, 4.0)
    top_scale = 10.0
    row_scale = jnp.exp(jax.random.uniform(row_key, (LENGTH,), jnp.float32) * jnp.log(top_scale))
    scale = jnp.concatenate([row_scale[None, :], jnp.ones((2, LENGTH), jnp.float32)], axis=0)
    return (base * scale[:, :, None]).astype(jnp.bfloat16)


def draw_short_weight(key, part):
    key = jax.random.fold_in(key, 23)
    base_key, column_key = jax.random.split(key)
    base = jnp.clip(jax.random.normal(base_key, (3, TAPS, D), jnp.float32), -3.0, 3.0)
    reach = 10.0
    position = jnp.arange(D, dtype=jnp.float32) / D
    spread = jnp.exp(jax.random.uniform(column_key, (D,), jnp.float32) * jnp.log(2.0))
    trend = jnp.exp(position * jnp.log(reach)) * spread
    scale = jnp.stack([trend, jnp.ones((D,), jnp.float32), jnp.ones((D,), jnp.float32)])
    return base * (1.0 / jnp.sqrt(7.0)) * scale[:, None, :]


def draw_spectrum(key, part):
    key = jax.random.fold_in(key, 37)
    memory_key, noise_key = jax.random.split(key)
    block_width = math.gcd(D, 256)
    block_count = D // block_width
    shortest = 32.0
    longest = 4.0 * LENGTH
    memory_span = shortest * jnp.exp(jax.random.uniform(memory_key, (D,), jnp.float32) * math.log(longest / shortest))
    energy_norm = jnp.sqrt(jnp.expm1(-2.0 / memory_span) / jnp.expm1(-2.0 * LENGTH / memory_span))
    lag_place = jnp.arange(LENGTH, dtype=jnp.int32).astype(jnp.float32).reshape(SHARDS, ROWS)
    outer_angle = (jnp.arange(2 * SHARDS, dtype=jnp.int32)[:, None] * jnp.arange(SHARDS, dtype=jnp.int32)[None, :] % (2 * SHARDS)).astype(jnp.float32) * (-2.0 * math.pi / (2 * SHARDS))
    inner_angle = (jnp.arange(ROWS, dtype=jnp.int32)[:, None] * jnp.arange(ROWS, dtype=jnp.int32)[None, :] % ROWS).astype(jnp.float32) * (-2.0 * math.pi / ROWS)
    turn_angle = (jnp.arange(2 * SHARDS, dtype=jnp.int32)[:, None] * jnp.arange(ROWS, dtype=jnp.int32)[None, :]).astype(jnp.float32) * (-2.0 * math.pi / SPAN)
    outer_cos = jnp.cos(outer_angle)
    outer_sin = jnp.sin(outer_angle)
    inner_cos = jnp.cos(inner_angle)
    inner_sin = jnp.sin(inner_angle)
    turn_cos = jnp.cos(turn_angle)[:, :, None]
    turn_sin = jnp.sin(turn_angle)[:, :, None]
    highest = lax.Precision.HIGHEST

    def one_block(inputs):
        block_index, memory_block, norm_block = inputs
        block_key = jax.random.fold_in(noise_key, block_index)
        noise_part = jnp.clip(jax.random.normal(block_key, (SHARDS, ROWS, block_width), jnp.float32), -4.0, 4.0)
        envelope = jnp.exp(-lag_place[:, :, None] / memory_block[None, None, :]) * norm_block[None, None, :]
        filter_taps = noise_part * envelope
        part_re = jnp.einsum('kn,nmc->kmc', outer_cos, filter_taps, precision=highest)
        part_im = jnp.einsum('kn,nmc->kmc', outer_sin, filter_taps, precision=highest)
        first_re = turn_cos * part_re - turn_sin * part_im
        first_im = turn_cos * part_im + turn_sin * part_re
        total_re = jnp.einsum('jm,kmc->kjc', inner_cos, first_re, precision=highest) - jnp.einsum('jm,kmc->kjc', inner_sin, first_im, precision=highest)
        total_im = jnp.einsum('jm,kmc->kjc', inner_cos, first_im, precision=highest) + jnp.einsum('jm,kmc->kjc', inner_sin, first_re, precision=highest)
        return jnp.stack([total_re, total_im]).astype(jnp.bfloat16)
    blocks = lax.map(one_block, (jnp.arange(block_count, dtype=jnp.int32), memory_span.reshape(block_count, block_width), energy_norm.reshape(block_count, block_width)))
    return jnp.transpose(blocks, (1, 2, 3, 0, 4)).reshape(2, 2 * SHARDS, ROWS, D)


def shard_levels(stream_key, extent, cuts, low, largest):
    level, own = 1.0, jax.random.fold_in(stream_key, 6)
    for dim, parts in cuts:
        draws = jnp.exp(jax.random.uniform(jax.random.fold_in(own, dim), (parts,), jnp.float32, low / len(cuts), largest / len(cuts)))
        level = level * jnp.repeat(draws, extent[dim] // parts).reshape([-1 if axis == dim else 1 for axis in range(len(extent))])
    return level


def setup_inputs(seed: int = 0) -> dict:
    arg_keys = jax.random.split(jax.random.key(seed), 6)
    proj = draw_proj(jax.random.fold_in(arg_keys[5], 71), 0)
    short_weight = draw_short_weight(jax.random.fold_in(arg_keys[5], 71), 0)
    spectrum = draw_spectrum(jax.random.fold_in(arg_keys[5], 71), 0)
    skip = jnp.clip(jnp.exp(math.log(1.5) - 1.60943787 * jax.random.uniform(arg_keys[3], (D,), jnp.float32) ** shard_levels(arg_keys[3], (D,), ((0, 8),), -0.2, 0.2)), 0.3, 1.5)
    gain = jnp.clip(1.0 + 0.1 * jax.random.normal(arg_keys[4], (D,), jnp.float32), 0.5, 1.5)
    return {"proj": proj, "short_weight": short_weight, "spectrum": spectrum, "skip": skip, "gain": gain}


epsilon = 1e-05

def dft_table(out_count, in_count, period, direction):
    product_index = jnp.arange(out_count, dtype=jnp.int32)[:, None] * jnp.arange(in_count, dtype=jnp.int32)[None, :] % period
    angle = product_index.astype(jnp.float32) * (direction * 2.0 * math.pi / period)
    return (jnp.cos(angle).astype(jnp.bfloat16), jnp.sin(angle).astype(jnp.bfloat16))

def twiddle_table(freq_index, place_index, span_size, direction):
    product_index = freq_index[:, None] * place_index[None, :]
    angle = product_index.astype(jnp.float32) * (direction * 2.0 * math.pi / span_size)
    return (jnp.cos(angle), jnp.sin(angle))

def rounded(value):
    return lax.optimization_barrier(value.astype(jnp.bfloat16)).astype(jnp.float32)

def reference(proj, short_weight, spectrum, skip, gain):
    outer_cos, outer_sin = dft_table(2 * SHARDS, SHARDS, 2 * SHARDS, -1.0)
    inner_cos, inner_sin = dft_table(ROWS, ROWS, ROWS, -1.0)
    back_cos, back_sin = dft_table(SHARDS, 2 * SHARDS, 2 * SHARDS, 1.0)
    outer_cos = outer_cos.astype(jnp.float32)
    outer_sin = outer_sin.astype(jnp.float32)
    inner_cos = inner_cos.astype(jnp.float32)
    inner_sin = inner_sin.astype(jnp.float32)
    back_cos = back_cos.astype(jnp.float32)
    back_sin = back_sin.astype(jnp.float32)
    turn_cos, turn_sin = twiddle_table(jnp.arange(2 * SHARDS, dtype=jnp.int32), jnp.arange(ROWS, dtype=jnp.int32), SPAN, -1.0)
    turn_cos = turn_cos[:, :, None]
    turn_sin = turn_sin[:, :, None]
    block_width = math.gcd(D, 256)
    block_count = D // block_width

    def one_block(block_index):
        start = (block_index * block_width).astype(jnp.int32)
        inputs = lax.dynamic_slice_in_dim(proj, start, block_width, 2).astype(jnp.float32)
        weights = lax.dynamic_slice_in_dim(short_weight, start, block_width, 2)
        filters = lax.dynamic_slice_in_dim(spectrum, start, block_width, 3).astype(jnp.float32)
        skip_part = lax.dynamic_slice_in_dim(skip, start, block_width, 0)
        padded = jnp.pad(inputs, ((0, 0), (TAPS - 1, 0), (0, 0)))
        shorts = jnp.zeros((3, LENGTH, block_width), jnp.float32)
        for tap_index in range(TAPS):
            offset = TAPS - 1 - tap_index
            shorts = shorts + weights[:, tap_index, None, :] * padded[:, offset:offset + LENGTH, :]
        gate = rounded(shorts[0])
        gated = rounded(shorts[1] * shorts[2])
        blocks = gated.reshape(SHARDS, ROWS, block_width)
        part_re = jnp.einsum('kn,nmc->kmc', outer_cos, blocks)
        part_im = jnp.einsum('kn,nmc->kmc', outer_sin, blocks)
        first_re = rounded(turn_cos * part_re - turn_sin * part_im)
        first_im = rounded(turn_cos * part_im + turn_sin * part_re)
        freq_re = jnp.einsum('jm,kmc->kjc', inner_cos, first_re) - jnp.einsum('jm,kmc->kjc', inner_sin, first_im)
        freq_im = jnp.einsum('jm,kmc->kjc', inner_cos, first_im) + jnp.einsum('jm,kmc->kjc', inner_sin, first_re)
        filtered_re = rounded(filters[0] * freq_re - filters[1] * freq_im)
        filtered_im = rounded(filters[0] * freq_im + filters[1] * freq_re)
        spread_re = jnp.einsum('jm,kjc->kmc', inner_cos, filtered_re) + jnp.einsum('jm,kjc->kmc', inner_sin, filtered_im)
        spread_im = jnp.einsum('jm,kjc->kmc', inner_cos, filtered_im) - jnp.einsum('jm,kjc->kmc', inner_sin, filtered_re)
        back_re = rounded(turn_cos * spread_re + turn_sin * spread_im)
        back_im = rounded(turn_cos * spread_im - turn_sin * spread_re)
        long_conv = (jnp.einsum('nk,kmc->nmc', back_cos, back_re) - jnp.einsum('nk,kmc->nmc', back_sin, back_im)) * (1.0 / SPAN)
        long_conv = long_conv.reshape(LENGTH, block_width)
        return gate * (long_conv + skip_part * gated)
    mixed = lax.map(one_block, jnp.arange(block_count, dtype=jnp.int32))
    power = lax.optimization_barrier(jnp.sum(mixed * mixed, axis=(0, 2))) / D
    scale = lax.rsqrt(power + epsilon)
    normed = (mixed * scale[None, :, None] * gain.reshape(block_count, 1, block_width)).astype(jnp.bfloat16)
    normed = jnp.transpose(normed, (1, 0, 2)).reshape(2 * SHARDS, ROWS // 2, D)
    return jnp.stack([normed[:SHARDS], normed[SHARDS:][::-1]], axis=1)
```

```python
import functools
import math

import jax
import jax.numpy as jnp
import ml_dtypes
import numpy as np
from jax import lax
from jax.experimental import pallas as pl
from jax.experimental.pallas import tpu as pltpu
from jax.sharding import PartitionSpec as P

MESH = pl.DeviceIdType.MESH
F32 = jnp.float32
BF16 = jnp.bfloat16

D = 8192
EPSILON = 1e-05
LENGTH = 16384
SHARDS = 32
CHANS = 8
ROWS = 512
WIDTH = 1024
OWN = 32
GROUP = 16
HALO = 16
TAPS = 7


def turn(numerator, period):
    angle = np.asarray(numerator % period, np.float64) * (2.0 * math.pi / period)
    return np.cos(angle), np.sin(angle)


@functools.cache
def tables():
    outer = np.arange(SHARDS)
    inner = np.arange(ROWS)
    eye = np.eye(GROUP)
    cos_k, sin_k = turn(np.outer(np.arange(256), inner), ROWS)
    spectrum_in = np.block([[cos_k, sin_k], [-sin_k, cos_k]])
    cos_f, sin_f = turn(np.outer(inner, inner), ROWS)
    forward = np.block([[cos_f, -sin_f], [sin_f, cos_f]])
    inverse = np.block([[cos_f, sin_f], [-sin_f, cos_f]])
    cos_s, sin_s = turn(np.outer(2 * outer + 1, outer), 64)
    cos_a, sin_a = turn(np.outer(4 * outer + 1, outer), 128)
    scale = 2.0 / LENGTH
    filter_outer = scale * np.block(
        [[cos_a @ cos_s.T, -cos_a @ sin_s.T], [-sin_a @ cos_s.T, sin_a @ sin_s.T]]
    )
    outer_in = np.concatenate([cos_a, -sin_a], axis=0)
    outer_out = np.concatenate([cos_a.T, -sin_a.T], axis=1) / LENGTH
    filter_turn = turn(np.outer(2 * outer + 1, inner), 2 * LENGTH)
    value_turn = turn(np.outer(4 * outer + 1, inner), 4 * LENGTH)
    value_turn = (value_turn[0], -value_turn[1])
    matrices = (
        spectrum_in,
        np.kron(filter_outer, eye),
        forward,
        np.kron(outer_in, eye),
        inverse,
        np.kron(outer_out, eye),
    )
    turns = [np.broadcast_to(t[:, None, :], (SHARDS, 8, ROWS)) for t in (*filter_turn, *value_turn)]
    return tuple(m.astype(ml_dtypes.bfloat16) for m in matrices) + tuple(
        np.ascontiguousarray(t, np.float32) for t in turns
    )


def dot(left, right):
    return jnp.dot(left, right, preferred_element_type=F32)


def rows_of(value):
    return value.reshape(SHARDS, 2, 8, value.shape[-1])


def kernel(
    proj,
    spectrum,
    weight,
    skip,
    gain,
    h_spectrum_in,
    h_filter_outer,
    h_forward,
    h_outer_in,
    h_inverse,
    h_outer_out,
    h_filter_cos,
    h_filter_sin,
    h_value_cos,
    h_value_sin,
    out,
    spec_local,
    proj_local,
    spec_send,
    gated_send,
    gate_send,
    spec_got,
    gated_got,
    gate_got,
    mixed_send,
    mixed_got,
    spectrum_in,
    filter_outer,
    forward,
    outer_in,
    inverse,
    outer_out,
    filter_cos,
    filter_sin,
    value_cos,
    value_sin,
    filter_freq,
    stacked_rows,
    stacked_lanes,
    unmixed,
    skip_own,
    power_send,
    power_got,
    load_sem,
    table_sem,
    halo_sem,
    send_sem,
    got_sem,
    power_send_sem,
    power_got_sem,
):
    me = lax.axis_index("seq")
    my_chan = lax.axis_index("chan")

    spec_load = pltpu.make_async_copy(spectrum.at[:, 1, pl.ds(0, 256), :], spec_local, load_sem.at[0])
    proj_load = pltpu.make_async_copy(proj, proj_local.at[:, pl.ds(HALO, ROWS), :], load_sem.at[1])
    spec_load.start()
    proj_load.start()
    loads = [
        pltpu.make_async_copy(source, target, table_sem.at[index])
        for index, (source, target) in enumerate(
            (
                (h_spectrum_in, spectrum_in),
                (h_filter_outer, filter_outer),
                (h_forward, forward),
                (h_outer_in, outer_in),
                (h_inverse, inverse),
                (h_outer_out, outer_out),
                (h_filter_cos, filter_cos),
                (h_filter_sin, filter_sin),
                (h_value_cos, value_cos),
                (h_value_sin, value_sin),
            )
        )
    ]
    for load in loads:
        load.start()

    barrier = pltpu.get_barrier_semaphore()

    @pl.loop(1, SHARDS)
    def _(k):
        pl.semaphore_signal(
            barrier, inc=1, device_id={"seq": lax.rem(me + k, SHARDS)}, device_id_type=MESH
        )

    @pl.loop(1, CHANS)
    def _(k):
        pl.semaphore_signal(
            barrier, inc=1, device_id={"chan": lax.rem(my_chan + k, CHANS)}, device_id_type=MESH
        )

    column = pl.multiple_of((me // 4) * 128, 128)
    wide = jnp.transpose(jnp.broadcast_to(skip[:, pl.ds(column, 128)], (128, 128)))
    unmixed[0, pl.ds(0, 128), pl.ds(0, 128)] = wide
    mine = unmixed[0, pl.ds(pl.multiple_of(lax.rem(me, 4) * OWN, OWN), OWN), pl.ds(0, 128)]
    skip_own[:, pl.ds(0, 128)] = mine
    skip_own[:, pl.ds(128, 128)] = mine

    pl.semaphore_wait(barrier, SHARDS - 1 + CHANS - 1)

    halo = pltpu.make_async_remote_copy(
        src_ref=proj.at[:, pl.ds(ROWS - HALO, HALO), :],
        dst_ref=proj_local.at[:, pl.ds(0, HALO), :],
        send_sem=halo_sem.at[0],
        recv_sem=halo_sem.at[1],
        device_id={"seq": lax.rem(me + 1, SHARDS)},
        device_id_type=MESH,
    )

    @pl.when(me < SHARDS - 1)
    def _():
        halo.start()

    def own_rows(device):
        return pl.ds(pl.multiple_of(device * OWN, OWN), OWN)

    def send_all(source, target, which):
        @pl.loop(1, SHARDS)
        def _(k):
            device = lax.rem(me + k, SHARDS)
            pltpu.make_async_remote_copy(
                src_ref=source.at[device],
                dst_ref=target.at[me],
                send_sem=send_sem.at[which],
                recv_sem=got_sem.at[which],
                device_id={"seq": device},
                device_id_type=MESH,
            ).start()

        target[me] = source[me]

    def wait_all(ref, sem):
        part = ref.at[pl.ds(0, SHARDS - 1)]
        pltpu.make_async_copy(part, part, sem).wait()

    spec_load.wait()

    @pl.loop(0, WIDTH // 128)
    def _(block):
        columns = pl.ds(pl.multiple_of(block * 128, 128), 128)
        for part in range(2):
            value = jnp.transpose(spec_local[part, :, columns].astype(F32)).astype(BF16)
            spec_send[pl.ds(block * 4, 4), :, pl.ds(part * 256, 256)] = value.reshape(4, OWN, 256)

    send_all(spec_send, spec_got, 0)

    proj_load.wait()

    @pl.when(me == 0)
    def _():
        proj_local[:, pl.ds(0, HALO), :] = jnp.zeros((3, HALO, WIDTH), BF16)

    @pl.when(me > 0)
    def _():
        halo.wait_recv()

    @pl.loop(0, WIDTH // 128)
    def _(block):
        columns = pl.ds(pl.multiple_of(block * 128, 128), 128)

        @pl.loop(0, ROWS // 128)
        def _(tile):
            start = pl.multiple_of(tile * 128, 128)
            shorts = []
            for feature in range(3):
                taken = proj_local[feature, pl.ds(start, 128 + HALO), columns].astype(F32)
                total = jnp.zeros((128, 128), F32)
                for tap in range(TAPS):
                    total = (
                        total
                        + weight[feature, pl.ds(tap, 1), columns] * taken[HALO - tap : HALO - tap + 128]
                    )
                shorts.append(total)
            places = pl.ds(start, 128)
            gate_send[pl.ds(block * 4, 4), :, places] = (
                jnp.transpose(shorts[0]).astype(BF16).reshape(4, OWN, 128)
            )
            gated_send[pl.ds(block * 4, 4), :, places] = (
                jnp.transpose(shorts[1] * shorts[2]).astype(BF16).reshape(4, OWN, 128)
            )

    send_all(gated_send, gated_got, 1)

    for load in loads:
        load.wait()
    wait_all(spec_got, got_sem.at[0])

    def turned(real, imag, cosine, sine, lanes, sign):
        real, imag = rows_of(real), rows_of(imag)
        c = cosine[:, :, lanes].reshape(SHARDS, 1, 8, 256)
        s = sine[:, :, lanes].reshape(SHARDS, 1, 8, 256)
        if sign > 0:
            new = (c * real - s * imag, c * imag + s * real)
        else:
            new = (c * real + s * imag, c * imag - s * real)
        return tuple(v.reshape(ROWS, 256).astype(BF16) for v in new)

    halves = (pl.ds(0, 256), pl.ds(256, 256))
    uppers = (pl.ds(512, 256), pl.ds(768, 256))
    top, bottom = pl.ds(0, ROWS), pl.ds(ROWS, ROWS)

    @pl.loop(0, OWN // GROUP)
    def _(group):
        chans = pl.ds(pl.multiple_of(group * GROUP, GROUP), GROUP)
        taken = spec_got[:, chans, :].reshape(ROWS, ROWS)
        for low, high in zip(halves, uppers):
            real, imag = dot(taken, spectrum_in[:, low]), dot(taken, spectrum_in[:, high])
            real, imag = turned(real, imag, filter_cos, filter_sin, low, 1)
            stacked_rows[top, low] = real
            stacked_rows[bottom, low] = imag
        for low, high in zip(halves, uppers):
            both = dot(filter_outer[...], stacked_rows[:, low])
            real, imag = turned(both[:ROWS], both[ROWS:], value_cos, value_sin, low, 1)
            stacked_lanes[:, low] = real
            stacked_lanes[:, high] = imag
        for lanes in (*halves, *uppers):
            filter_freq[group, :, lanes] = dot(stacked_lanes[...], forward[:, lanes])

    wait_all(gated_got, got_sem.at[1])
    send_all(gate_send, gate_got, 2)

    @pl.loop(0, OWN // GROUP)
    def _(group):
        chans = pl.ds(pl.multiple_of(group * GROUP, GROUP), GROUP)
        for low, high in zip(halves, uppers):
            both = dot(outer_in[...], gated_got[:, chans, low].reshape(ROWS, 256))
            real, imag = turned(both[:ROWS], both[ROWS:], value_cos, value_sin, low, 1)
            stacked_lanes[:, low] = real
            stacked_lanes[:, high] = imag
        for low, high in zip(halves, uppers):
            real, imag = dot(stacked_lanes[...], forward[:, low]), dot(stacked_lanes[...], forward[:, high])
            f_real, f_imag = filter_freq[group, :, low], filter_freq[group, :, high]
            stacked_rows[top, low] = (f_real * real - f_imag * imag).astype(BF16)
            stacked_rows[bottom, low] = (f_real * imag + f_imag * real).astype(BF16)
        for low, high in zip(halves, uppers):
            real = dot(stacked_rows[top, :], inverse[top, low]) + dot(
                stacked_rows[bottom, :], inverse[bottom, low]
            )
            imag = dot(stacked_rows[top, :], inverse[top, high]) + dot(
                stacked_rows[bottom, :], inverse[bottom, high]
            )
            real, imag = turned(real, imag, value_cos, value_sin, low, -1)
            stacked_lanes[:, low] = real
            stacked_lanes[:, high] = imag
        for low, high in zip(halves, uppers):
            value = dot(outer_out[:, top], stacked_lanes[:, low]) + dot(
                outer_out[:, bottom], stacked_lanes[:, high]
            )
            own = gated_got[:, chans, low].astype(F32)
            unmixed[group, :, low] = (
                value.reshape(SHARDS, GROUP, 256) + skip_own[chans, :][None] * own
            ).reshape(ROWS, 256)

    wait_all(gate_got, got_sem.at[2])

    for side in range(2):

        @pl.loop(0, OWN // GROUP)
        def _(group):
            chans = pl.ds(pl.multiple_of(group * GROUP, GROUP), GROUP)
            for half, lanes in enumerate(halves):
                value = unmixed[group, pl.ds(side * 256, 256), lanes].reshape(16, GROUP, 256)
                value = (gate_got[pl.ds(side * 16, 16), chans, lanes].astype(F32) * value).astype(BF16)
                for index in range(16):
                    device = 2 * index + half if side == 0 else 31 - 2 * index - half
                    mixed_send[side, device, chans, :] = value[index]

        send_all(mixed_send.at[side], mixed_got.at[side], 3 + side)

    for side in range(2):
        wait_all(mixed_got.at[side], got_sem.at[3 + side])

        def squares(block, total):
            value = mixed_got[side, pl.ds(block * 4, 4), :, :].astype(F32)
            value = (value * value).reshape(16, 8, 256)
            return total + jnp.sum(value, axis=0)

        power = lax.fori_loop(0, WIDTH // 128, squares, jnp.zeros((8, 256), F32))
        power_send[side] = power
        power_got[side, my_chan] = power

        @pl.loop(1, CHANS)
        def _(k):
            pltpu.make_async_remote_copy(
                src_ref=power_send.at[side],
                dst_ref=power_got.at[side, my_chan],
                send_sem=power_send_sem.at[side],
                recv_sem=power_got_sem.at[side],
                device_id={"chan": lax.rem(my_chan + k, CHANS)},
                device_id_type=MESH,
            ).start()

        @pl.loop(0, WIDTH // 128)
        def _(block):
            value = mixed_got[side, pl.ds(block * 4, 4), :, :].reshape(128, 256).astype(F32)
            columns = pl.ds(pl.multiple_of(block * 128, 128), 128)
            out[pl.ds(side * 256, 256), columns] = jnp.transpose(value).astype(BF16)

    for side in range(2):
        part = power_got.at[side, pl.ds(0, CHANS - 1)]
        pltpu.make_async_copy(part, part, power_got_sem.at[side]).wait()
        power = jnp.sum(jnp.sum(power_got[side], axis=0), axis=0, keepdims=True)
        scale = lax.rsqrt(power * (1.0 / D) + EPSILON)
        scale = jnp.transpose(jnp.broadcast_to(scale, (128, 256)))

        @pl.loop(0, WIDTH // 128)
        def _(block):
            columns = pl.ds(pl.multiple_of(block * 128, 128), 128)
            rows = pl.ds(side * 256, 256)
            out[rows, columns] = (out[rows, columns].astype(F32) * scale * gain[:, columns]).astype(BF16)

    @pl.when(me < SHARDS - 1)
    def _():
        halo.wait_send()

    wait_all(spec_send, send_sem.at[0])
    wait_all(gated_send, send_sem.at[1])
    wait_all(gate_send, send_sem.at[2])
    for side in range(2):
        wait_all(mixed_send.at[side], send_sem.at[3 + side])
        part = power_got.at[side, pl.ds(0, CHANS - 1)]
        pltpu.make_async_copy(part, part, power_send_sem.at[side]).wait()


def body(proj, short_weight, spectrum, skip, gain):
    constants = tables()
    held = [pltpu.VMEM(c.shape, c.dtype) for c in constants]
    whole = (SHARDS, OWN, ROWS)
    anywhere = pl.BlockSpec(memory_space=pl.ANY)
    inside = pl.BlockSpec(memory_space=pltpu.VMEM)
    value = pl.pallas_call(
        kernel,
        out_shape=jax.ShapeDtypeStruct((ROWS, WIDTH), BF16),
        in_specs=[anywhere, anywhere, inside, inside, inside] + [anywhere] * len(constants),
        out_specs=inside,
        scratch_shapes=[
            pltpu.VMEM((2, 256, WIDTH), BF16),
            pltpu.VMEM((3, HALO + ROWS, WIDTH), BF16),
            pltpu.VMEM(whole, BF16),
            pltpu.VMEM(whole, BF16),
            pltpu.VMEM(whole, BF16),
            pltpu.VMEM(whole, BF16),
            pltpu.VMEM(whole, BF16),
            pltpu.VMEM(whole, BF16),
            pltpu.VMEM((2, SHARDS, OWN, 256), BF16),
            pltpu.VMEM((2, SHARDS, OWN, 256), BF16),
            *held,
            pltpu.VMEM((OWN // GROUP, ROWS, 2 * ROWS), F32),
            pltpu.VMEM((2 * ROWS, ROWS), BF16),
            pltpu.VMEM((ROWS, 2 * ROWS), BF16),
            pltpu.VMEM((OWN // GROUP, ROWS, ROWS), F32),
            pltpu.VMEM((OWN, 256), F32),
            pltpu.VMEM((2, 8, 256), F32),
            pltpu.VMEM((2, CHANS, 8, 256), F32),
            pltpu.SemaphoreType.DMA((2,)),
            pltpu.SemaphoreType.DMA((len(constants),)),
            pltpu.SemaphoreType.DMA((2,)),
            pltpu.SemaphoreType.DMA((5,)),
            pltpu.SemaphoreType.DMA((5,)),
            pltpu.SemaphoreType.DMA((2,)),
            pltpu.SemaphoreType.DMA((2,)),
        ],
        compiler_params=pltpu.CompilerParams(
            collective_id=0, has_side_effects=True, vmem_limit_bytes=56 * 2**20
        ),
    )(proj, spectrum, short_weight, skip[None], gain[None], *(jnp.asarray(c) for c in constants))
    return value.reshape(1, 2, ROWS // 2, WIDTH)


def solution(mesh):
    placed = (
        P(None, "seq", "chan"),
        P(None, None, "chan"),
        P(None, "seq", None, "chan"),
        P("chan"),
        P("chan"),
    )
    return jax.shard_map(
        body, mesh=mesh, in_specs=placed, out_specs=P("seq", None, None, "chan"), check_vma=False
    )
```

```python
import functools
import math

import jax
import jax.numpy as jnp
import ml_dtypes
import numpy as np
from jax import lax
from jax.experimental import pallas as pl
from jax.experimental.pallas import tpu as pltpu
from jax.sharding import PartitionSpec as P

MESH = pl.DeviceIdType.MESH
F32 = jnp.float32
BF16 = jnp.bfloat16

D = 8192
EPSILON = 1e-05
LENGTH = 16384
SHARDS = 32
CHANS = 8
ROWS = 512
WIDTH = 1024
OWN = 32
GROUP = 16
GROUPS = OWN // GROUP
HALO = 16
TAPS = 7
SPECTRUM, GATED, GATE, MIXED, EXCHANGES = 0, 1, 3, 5, 9


def turn(numerator, period):
    angle = np.asarray(numerator % period, np.float64) * (2.0 * math.pi / period)
    return np.cos(angle), np.sin(angle)


@functools.cache
def tables():
    outer = np.arange(SHARDS)
    inner = np.arange(ROWS)
    eye = np.eye(GROUP)
    cos_k, sin_k = turn(np.outer(np.arange(256), inner), ROWS)
    spectrum_in = np.block([[cos_k, sin_k], [-sin_k, cos_k]])
    cos_f, sin_f = turn(np.outer(inner, inner), ROWS)
    forward = np.block([[cos_f, -sin_f], [sin_f, cos_f]])
    inverse = np.block([[cos_f, sin_f], [-sin_f, cos_f]])
    cos_s, sin_s = turn(np.outer(2 * outer + 1, outer), 64)
    cos_a, sin_a = turn(np.outer(4 * outer + 1, outer), 128)
    scale = 2.0 / LENGTH
    filter_outer = scale * np.block(
        [[cos_a @ cos_s.T, -cos_a @ sin_s.T], [-sin_a @ cos_s.T, sin_a @ sin_s.T]]
    )
    outer_in = np.concatenate([cos_a, -sin_a], axis=0)
    outer_out = np.concatenate([cos_a.T, -sin_a.T], axis=1) / LENGTH
    filter_turn = turn(np.outer(2 * outer + 1, inner), 2 * LENGTH)
    value_turn = turn(np.outer(4 * outer + 1, inner), 4 * LENGTH)
    value_turn = (value_turn[0], -value_turn[1])
    matrices = (
        spectrum_in,
        np.kron(filter_outer, eye),
        forward,
        np.kron(outer_in, eye),
        inverse,
        np.kron(outer_out, eye),
    )
    turns = [np.broadcast_to(t[:, None, :], (SHARDS, 8, ROWS)) for t in (*filter_turn, *value_turn)]
    return tuple(m.astype(ml_dtypes.bfloat16) for m in matrices) + tuple(
        np.ascontiguousarray(t, np.float32) for t in turns
    )


def dot(left, right):
    return jnp.dot(left, right, preferred_element_type=F32)


def rows_of(value):
    return value.reshape(SHARDS, 2, 8, value.shape[-1])


def kernel(
    proj,
    spectrum,
    weight,
    skip,
    gain,
    h_spectrum_in,
    h_filter_outer,
    h_forward,
    h_outer_in,
    h_inverse,
    h_outer_out,
    h_filter_cos,
    h_filter_sin,
    h_value_cos,
    h_value_sin,
    out,
    spec_local,
    proj_local,
    spec_send,
    gated_send,
    gate_send,
    spec_got,
    gated_got,
    gate_got,
    mixed_send,
    mixed_got,
    spectrum_in,
    filter_outer,
    forward,
    outer_in,
    inverse,
    outer_out,
    filter_cos,
    filter_sin,
    value_cos,
    value_sin,
    filter_freq,
    stacked_rows,
    stacked_lanes,
    unmixed,
    skip_own,
    power_send,
    power_got,
    load_sem,
    table_sem,
    halo_sem,
    send_sem,
    got_sem,
    power_send_sem,
    power_got_sem,
):
    me = lax.axis_index("seq")
    my_chan = lax.axis_index("chan")

    spec_load = pltpu.make_async_copy(spectrum.at[:, 1, pl.ds(0, 256), :], spec_local, load_sem.at[0])
    proj_load = pltpu.make_async_copy(proj, proj_local.at[:, pl.ds(HALO, ROWS), :], load_sem.at[1])
    spec_load.start()
    barrier = pltpu.get_barrier_semaphore()

    @pl.loop(1, SHARDS)
    def _(k):
        pl.semaphore_signal(
            barrier, inc=1, device_id={"seq": lax.rem(me + k, SHARDS)}, device_id_type=MESH
        )

    @pl.loop(1, CHANS)
    def _(k):
        pl.semaphore_signal(
            barrier, inc=1, device_id={"chan": lax.rem(my_chan + k, CHANS)}, device_id_type=MESH
        )

    proj_load.start()
    loads = [
        pltpu.make_async_copy(source, target, table_sem.at[index])
        for index, (source, target) in enumerate(
            (
                (h_spectrum_in, spectrum_in),
                (h_filter_outer, filter_outer),
                (h_forward, forward),
                (h_outer_in, outer_in),
                (h_inverse, inverse),
                (h_outer_out, outer_out),
                (h_filter_cos, filter_cos),
                (h_filter_sin, filter_sin),
                (h_value_cos, value_cos),
                (h_value_sin, value_sin),
            )
        )
    ]
    for load in loads:
        load.start()

    pl.semaphore_wait(barrier, SHARDS - 1 + CHANS - 1)

    halo = pltpu.make_async_remote_copy(
        src_ref=proj.at[:, pl.ds(ROWS - HALO, HALO), :],
        dst_ref=proj_local.at[:, pl.ds(0, HALO), :],
        send_sem=halo_sem.at[0],
        recv_sem=halo_sem.at[1],
        device_id={"seq": lax.rem(me + 1, SHARDS)},
        device_id_type=MESH,
    )

    @pl.when(me < SHARDS - 1)
    def _():
        halo.start()

    def send_one(source, target, device, which):
        pltpu.make_async_remote_copy(
            src_ref=source.at[device],
            dst_ref=target.at[me],
            send_sem=send_sem.at[which],
            recv_sem=got_sem.at[which],
            device_id={"seq": device},
            device_id_type=MESH,
        ).start()

    def send_all(source, target, which):
        @pl.loop(1, SHARDS)
        def _(k):
            send_one(source, target, lax.rem(me + k, SHARDS), which)

    def wait_all(ref, sem):
        part = ref.at[pl.ds(0, SHARDS - 1)]
        pltpu.make_async_copy(part, part, sem).wait()

    spec_load.wait()

    @pl.loop(0, WIDTH // 128)
    def _(step):
        block = lax.rem(me // 4 + step, WIDTH // 128)
        columns = pl.ds(pl.multiple_of(block * 128, 128), 128)
        for part in range(2):
            value = jnp.transpose(spec_local[part, :, columns].astype(F32)).astype(BF16)
            spec_send[pl.ds(block * 4, 4), :, pl.ds(part * 256, 256)] = value.reshape(4, OWN, 256)

        @pl.loop(0, 4)
        def _(k):
            device = block * 4 + lax.rem(me + k, 4)

            @pl.when(device != me)
            def _():
                send_one(spec_send, spec_got, device, SPECTRUM)

    spec_got[me] = spec_send[me]

    column = pl.multiple_of((me // 4) * 128, 128)
    wide = jnp.transpose(jnp.broadcast_to(skip[:, pl.ds(column, 128)], (128, 128)))
    unmixed[pl.ds(0, 128), pl.ds(0, 128)] = wide
    mine = unmixed[pl.ds(pl.multiple_of(lax.rem(me, 4) * OWN, OWN), OWN), pl.ds(0, 128)]
    skip_own[:, pl.ds(0, 128)] = mine
    skip_own[:, pl.ds(128, 128)] = mine

    proj_load.wait()

    @pl.when(me == 0)
    def _():
        proj_local[:, pl.ds(0, HALO), :] = jnp.zeros((3, HALO, WIDTH), BF16)

    @pl.when(me > 0)
    def _():
        halo.wait_recv()

    @pl.loop(0, WIDTH // 128)
    def _(block):
        columns = pl.ds(pl.multiple_of(block * 128, 128), 128)

        @pl.loop(0, ROWS // 128)
        def _(tile):
            start = pl.multiple_of(tile * 128, 128)
            shorts = []
            for feature in range(3):
                taken = proj_local[feature, pl.ds(start, 128 + HALO), columns].astype(F32)
                total = jnp.zeros((128, 128), F32)
                for tap in range(TAPS):
                    total = (
                        total
                        + weight[feature, pl.ds(tap, 1), columns] * taken[HALO - tap : HALO - tap + 128]
                    )
                shorts.append(total)
            places = pl.ds(start, 128)
            gate_send[pl.ds(block * 4, 4), :, places] = (
                jnp.transpose(shorts[0]).astype(BF16).reshape(4, OWN, 128)
            )
            gated_send[pl.ds(block * 4, 4), :, places] = (
                jnp.transpose(shorts[1] * shorts[2]).astype(BF16).reshape(4, OWN, 128)
            )

    gated_got[me] = gated_send[me]
    gate_got[me] = gate_send[me]
    for group in range(GROUPS):
        chans = pl.ds(group * GROUP, GROUP)
        send_all(gated_send.at[:, chans, :], gated_got.at[:, chans, :], GATED + group)
        send_all(gate_send.at[:, chans, :], gate_got.at[:, chans, :], GATE + group)

    for load in loads:
        load.wait()
    wait_all(spec_got, got_sem.at[SPECTRUM])

    def turned(real, imag, cosine, sine, lanes, sign):
        real, imag = rows_of(real), rows_of(imag)
        c = cosine[:, :, lanes].reshape(SHARDS, 1, 8, 256)
        s = sine[:, :, lanes].reshape(SHARDS, 1, 8, 256)
        if sign > 0:
            new = (c * real - s * imag, c * imag + s * real)
        else:
            new = (c * real + s * imag, c * imag - s * real)
        return tuple(v.reshape(ROWS, 256).astype(BF16) for v in new)

    halves = (pl.ds(0, 256), pl.ds(256, 256))
    uppers = (pl.ds(512, 256), pl.ds(768, 256))
    top, bottom = pl.ds(0, ROWS), pl.ds(ROWS, ROWS)

    @pl.loop(0, GROUPS)
    def _(group):
        chans = pl.ds(pl.multiple_of(group * GROUP, GROUP), GROUP)
        taken = spec_got[:, chans, :].reshape(ROWS, ROWS)
        for low, high in zip(halves, uppers):
            real, imag = dot(taken, spectrum_in[:, low]), dot(taken, spectrum_in[:, high])
            real, imag = turned(real, imag, filter_cos, filter_sin, low, 1)
            stacked_rows[top, low] = real
            stacked_rows[bottom, low] = imag
        for low, high in zip(halves, uppers):
            both = dot(filter_outer[...], stacked_rows[:, low])
            real, imag = turned(both[:ROWS], both[ROWS:], value_cos, value_sin, low, 1)
            stacked_lanes[:, low] = real
            stacked_lanes[:, high] = imag
        for lanes in (*halves, *uppers):
            filter_freq[group, :, lanes] = dot(stacked_lanes[...], forward[:, lanes])

    @pl.loop(0, GROUPS)
    def _(group):
        chans = pl.ds(pl.multiple_of(group * GROUP, GROUP), GROUP)
        wait_all(gated_got.at[:, chans, :], got_sem.at[GATED + group])
        for low, high in zip(halves, uppers):
            both = dot(outer_in[...], gated_got[:, chans, low].reshape(ROWS, 256))
            real, imag = turned(both[:ROWS], both[ROWS:], value_cos, value_sin, low, 1)
            stacked_lanes[:, low] = real
            stacked_lanes[:, high] = imag
        for low, high in zip(halves, uppers):
            real, imag = dot(stacked_lanes[...], forward[:, low]), dot(stacked_lanes[...], forward[:, high])
            f_real, f_imag = filter_freq[group, :, low], filter_freq[group, :, high]
            stacked_rows[top, low] = (f_real * real - f_imag * imag).astype(BF16)
            stacked_rows[bottom, low] = (f_real * imag + f_imag * real).astype(BF16)
        for low, high in zip(halves, uppers):
            real = dot(stacked_rows[top, :], inverse[top, low]) + dot(
                stacked_rows[bottom, :], inverse[bottom, low]
            )
            imag = dot(stacked_rows[top, :], inverse[top, high]) + dot(
                stacked_rows[bottom, :], inverse[bottom, high]
            )
            real, imag = turned(real, imag, value_cos, value_sin, low, -1)
            stacked_lanes[:, low] = real
            stacked_lanes[:, high] = imag
        for low, high in zip(halves, uppers):
            value = dot(outer_out[:, top], stacked_lanes[:, low]) + dot(
                outer_out[:, bottom], stacked_lanes[:, high]
            )
            own = gated_got[:, chans, low].astype(F32)
            unmixed[:, low] = (
                value.reshape(SHARDS, GROUP, 256) + skip_own[chans, :][None] * own
            ).reshape(ROWS, 256)

        wait_all(gate_got.at[:, chans, :], got_sem.at[GATE + group])
        for side in range(2):
            for half, lanes in enumerate(halves):
                value = unmixed[pl.ds(side * 256, 256), lanes].reshape(16, GROUP, 256)
                value = (gate_got[pl.ds(side * 16, 16), chans, lanes].astype(F32) * value).astype(BF16)
                for index in range(16):
                    device = 2 * index + half if side == 0 else 31 - 2 * index - half
                    mixed_send[side, device, chans, :] = value[index]
            mixed_got[side, me, chans, :] = mixed_send[side, me, chans, :]
            send_all(
                mixed_send.at[side, :, chans, :],
                mixed_got.at[side, :, chans, :],
                MIXED + 2 * group + side,
            )

    for side in range(2):
        for group in range(GROUPS):
            wait_all(
                mixed_got.at[side, :, pl.ds(group * GROUP, GROUP), :],
                got_sem.at[MIXED + 2 * group + side],
            )

        def squares(block, total):
            value = mixed_got[side, pl.ds(block * 4, 4), :, :].astype(F32)
            value = (value * value).reshape(16, 8, 256)
            return total + jnp.sum(value, axis=0)

        power = lax.fori_loop(0, WIDTH // 128, squares, jnp.zeros((8, 256), F32))
        power_send[side] = power
        power_got[side, my_chan] = power

        @pl.loop(1, CHANS)
        def _(k):
            pltpu.make_async_remote_copy(
                src_ref=power_send.at[side],
                dst_ref=power_got.at[side, my_chan],
                send_sem=power_send_sem.at[side],
                recv_sem=power_got_sem.at[side],
                device_id={"chan": lax.rem(my_chan + k, CHANS)},
                device_id_type=MESH,
            ).start()

        @pl.loop(0, WIDTH // 128)
        def _(block):
            value = mixed_got[side, pl.ds(block * 4, 4), :, :].reshape(128, 256).astype(F32)
            columns = pl.ds(pl.multiple_of(block * 128, 128), 128)
            out[pl.ds(side * 256, 256), columns] = jnp.transpose(value).astype(BF16)

    for side in range(2):
        part = power_got.at[side, pl.ds(0, CHANS - 1)]
        pltpu.make_async_copy(part, part, power_got_sem.at[side]).wait()
        power = jnp.sum(jnp.sum(power_got[side], axis=0), axis=0, keepdims=True)
        scale = lax.rsqrt(power * (1.0 / D) + EPSILON)
        scale = jnp.transpose(jnp.broadcast_to(scale, (128, 256)))

        @pl.loop(0, WIDTH // 128)
        def _(block):
            columns = pl.ds(pl.multiple_of(block * 128, 128), 128)
            rows = pl.ds(side * 256, 256)
            out[rows, columns] = (out[rows, columns].astype(F32) * scale * gain[:, columns]).astype(BF16)

    @pl.when(me < SHARDS - 1)
    def _():
        halo.wait_send()

    wait_all(spec_send, send_sem.at[SPECTRUM])
    for group in range(GROUPS):
        chans = pl.ds(group * GROUP, GROUP)
        wait_all(gated_send.at[:, chans, :], send_sem.at[GATED + group])
        wait_all(gate_send.at[:, chans, :], send_sem.at[GATE + group])
        for side in range(2):
            wait_all(mixed_send.at[side, :, chans, :], send_sem.at[MIXED + 2 * group + side])
    for side in range(2):
        part = power_got.at[side, pl.ds(0, CHANS - 1)]
        pltpu.make_async_copy(part, part, power_send_sem.at[side]).wait()


def body(proj, short_weight, spectrum, skip, gain):
    constants = tables()
    held = [pltpu.VMEM(c.shape, c.dtype) for c in constants]
    whole = (SHARDS, OWN, ROWS)
    anywhere = pl.BlockSpec(memory_space=pl.ANY)
    inside = pl.BlockSpec(memory_space=pltpu.VMEM)
    value = pl.pallas_call(
        kernel,
        out_shape=jax.ShapeDtypeStruct((ROWS, WIDTH), BF16),
        in_specs=[anywhere, anywhere, inside, inside, inside] + [anywhere] * len(constants),
        out_specs=inside,
        scratch_shapes=[
            pltpu.VMEM((2, 256, WIDTH), BF16),
            pltpu.VMEM((3, HALO + ROWS, WIDTH), BF16),
            pltpu.VMEM(whole, BF16),
            pltpu.VMEM(whole, BF16),
            pltpu.VMEM(whole, BF16),
            pltpu.VMEM(whole, BF16),
            pltpu.VMEM(whole, BF16),
            pltpu.VMEM(whole, BF16),
            pltpu.VMEM((2, SHARDS, OWN, 256), BF16),
            pltpu.VMEM((2, SHARDS, OWN, 256), BF16),
            *held,
            pltpu.VMEM((GROUPS, ROWS, 2 * ROWS), F32),
            pltpu.VMEM((2 * ROWS, ROWS), BF16),
            pltpu.VMEM((ROWS, 2 * ROWS), BF16),
            pltpu.VMEM((ROWS, ROWS), F32),
            pltpu.VMEM((OWN, 256), F32),
            pltpu.VMEM((2, 8, 256), F32),
            pltpu.VMEM((2, CHANS, 8, 256), F32),
            pltpu.SemaphoreType.DMA((2,)),
            pltpu.SemaphoreType.DMA((len(constants),)),
            pltpu.SemaphoreType.DMA((2,)),
            pltpu.SemaphoreType.DMA((EXCHANGES,)),
            pltpu.SemaphoreType.DMA((EXCHANGES,)),
            pltpu.SemaphoreType.DMA((2,)),
            pltpu.SemaphoreType.DMA((2,)),
        ],
        compiler_params=pltpu.CompilerParams(
            collective_id=0, has_side_effects=True, vmem_limit_bytes=56 * 2**20
        ),
    )(proj, spectrum, short_weight, skip[None], gain[None], *(jnp.asarray(c) for c in constants))
    return value.reshape(1, 2, ROWS // 2, WIDTH)


def solution(mesh):
    placed = (
        P(None, "seq", "chan"),
        P(None, None, "chan"),
        P(None, "seq", None, "chan"),
        P("chan"),
        P("chan"),
    )
    return jax.shard_map(
        body, mesh=mesh, in_specs=placed, out_specs=P("seq", None, None, "chan"), check_vma=False
    )
```

```python
import functools
import math

import jax
import jax.numpy as jnp
import ml_dtypes
import numpy as np
from jax import lax
from jax.experimental import pallas as pl
from jax.experimental.pallas import tpu as pltpu
from jax.sharding import PartitionSpec as P

MESH = pl.DeviceIdType.MESH
F32 = jnp.float32
BF16 = jnp.bfloat16

D = 8192
EPSILON = 1e-05
LENGTH = 16384
SHARDS = 32
CHANS = 8
ROWS = 512
WIDTH = 1024
OWN = 32
GROUP = 16
GROUPS = OWN // GROUP
HALO = 16
TAPS = 7
SPECTRUM, GATED, GATE, MIXED, POWER, EXCHANGES = 0, 1, 3, 5, 9, 10


def turn(numerator, period):
    angle = np.asarray(numerator % period, np.float64) * (2.0 * math.pi / period)
    return np.cos(angle), np.sin(angle)


@functools.cache
def tables():
    outer = np.arange(SHARDS)
    inner = np.arange(ROWS)
    eye = np.eye(GROUP)
    cos_k, sin_k = turn(np.outer(np.arange(256), inner), ROWS)
    spectrum_in = np.block([[cos_k, sin_k], [-sin_k, cos_k]])
    cos_f, sin_f = turn(np.outer(inner, inner), ROWS)
    forward = np.block([[cos_f, -sin_f], [sin_f, cos_f]])
    inverse = np.block([[cos_f, sin_f], [-sin_f, cos_f]])
    cos_s, sin_s = turn(np.outer(2 * outer + 1, outer), 64)
    cos_a, sin_a = turn(np.outer(4 * outer + 1, outer), 128)
    scale = 2.0 / LENGTH
    filter_outer = scale * np.block(
        [[cos_a @ cos_s.T, -cos_a @ sin_s.T], [-sin_a @ cos_s.T, sin_a @ sin_s.T]]
    )
    outer_in = np.concatenate([cos_a, -sin_a], axis=0)
    outer_out = np.concatenate([cos_a.T, -sin_a.T], axis=1) / LENGTH
    filter_turn = turn(np.outer(2 * outer + 1, inner), 2 * LENGTH)
    value_turn = turn(np.outer(4 * outer + 1, inner), 4 * LENGTH)
    value_turn = (value_turn[0], -value_turn[1])
    matrices = (
        spectrum_in,
        np.kron(filter_outer, eye),
        forward,
        np.kron(outer_in, eye),
        inverse,
        np.kron(outer_out, eye),
    )
    turns = [np.broadcast_to(t[:, None, :], (SHARDS, 8, ROWS)) for t in (*filter_turn, *value_turn)]
    return tuple(m.astype(ml_dtypes.bfloat16) for m in matrices) + tuple(
        np.ascontiguousarray(t, np.float32) for t in turns
    )


def dot(left, right):
    return jnp.dot(left, right, preferred_element_type=F32)


def rows_of(value):
    return value.reshape(SHARDS, 2, 8, value.shape[-1])


def kernel(
    proj,
    spectrum,
    h_weight,
    h_skip,
    h_gain,
    h_spectrum_in,
    h_filter_outer,
    h_forward,
    h_outer_in,
    h_inverse,
    h_outer_out,
    h_filter_cos,
    h_filter_sin,
    h_value_cos,
    h_value_sin,
    h_out,
    weight,
    skip,
    gain,
    out,
    spec_local,
    proj_local,
    spec_send,
    gated_send,
    gate_send,
    spec_got,
    gated_got,
    gate_got,
    mixed_send,
    mixed_got,
    spectrum_in,
    filter_outer,
    forward,
    outer_in,
    inverse,
    outer_out,
    filter_cos,
    filter_sin,
    value_cos,
    value_sin,
    filter_freq,
    stacked_rows,
    stacked_lanes,
    unmixed,
    skip_own,
    part_send,
    part_got,
    power_send,
    power_got,
    scales,
    load_sem,
    table_sem,
    halo_sem,
    send_sem,
    got_sem,
    power_sem,
):
    me = lax.axis_index("seq")
    my_chan = lax.axis_index("chan")

    spec_load = pltpu.make_async_copy(spectrum.at[:, 1, pl.ds(0, 256), :], spec_local, load_sem.at[0])
    proj_load = pltpu.make_async_copy(proj, proj_local.at[:, pl.ds(HALO, ROWS), :], load_sem.at[1])
    spec_load.start()
    barrier = pltpu.get_barrier_semaphore()

    @pl.loop(1, SHARDS)
    def _(k):
        pl.semaphore_signal(
            barrier, inc=1, device_id={"seq": lax.rem(me + k, SHARDS)}, device_id_type=MESH
        )

    @pl.loop(1, CHANS)
    def _(k):
        pl.semaphore_signal(
            barrier, inc=1, device_id={"chan": lax.rem(my_chan + k, CHANS)}, device_id_type=MESH
        )

    pl.semaphore_wait(barrier, SHARDS - 1 + CHANS - 1)

    halo = pltpu.make_async_remote_copy(
        src_ref=proj.at[:, pl.ds(ROWS - HALO, HALO), :],
        dst_ref=proj_local.at[:, pl.ds(0, HALO), :],
        send_sem=halo_sem.at[0],
        recv_sem=halo_sem.at[1],
        device_id={"seq": lax.rem(me + 1, SHARDS)},
        device_id_type=MESH,
    )

    @pl.when(me < SHARDS - 1)
    def _():
        halo.start()

    def send_one(source, target, device, which):
        pltpu.make_async_remote_copy(
            src_ref=source.at[device],
            dst_ref=target.at[me],
            send_sem=send_sem.at[which],
            recv_sem=got_sem.at[which],
            device_id={"seq": device},
            device_id_type=MESH,
        ).start()

    def send_all(source, target, which):
        @pl.loop(1, SHARDS)
        def _(k):
            send_one(source, target, lax.rem(me + k, SHARDS), which)

    def wait_all(ref, sem):
        part = ref.at[pl.ds(0, SHARDS - 1)]
        pltpu.make_async_copy(part, part, sem).wait()

    spec_load.wait()
    proj_load.start()
    loads = [
        pltpu.make_async_copy(source, target, table_sem.at[index])
        for index, (source, target) in enumerate(
            (
                (h_weight, weight),
                (h_skip, skip),
                (h_gain, gain),
                (h_spectrum_in, spectrum_in),
                (h_filter_outer, filter_outer),
                (h_forward, forward),
                (h_outer_in, outer_in),
                (h_inverse, inverse),
                (h_outer_out, outer_out),
                (h_filter_cos, filter_cos),
                (h_filter_sin, filter_sin),
                (h_value_cos, value_cos),
                (h_value_sin, value_sin),
            )
        )
    ]
    for load in loads:
        load.start()

    @pl.loop(0, WIDTH // 128)
    def _(step):
        block = lax.rem(me // 4 + step, WIDTH // 128)
        columns = pl.ds(pl.multiple_of(block * 128, 128), 128)
        for part in range(2):
            value = jnp.transpose(spec_local[part, :, columns].astype(F32)).astype(BF16)
            spec_send[pl.ds(block * 4, 4), :, pl.ds(part * 256, 256)] = value.reshape(4, OWN, 256)

        @pl.loop(0, 4)
        def _(k):
            device = block * 4 + lax.rem(me + k, 4)

            @pl.when(device != me)
            def _():
                send_one(spec_send, spec_got, device, SPECTRUM)

    spec_got[me] = spec_send[me]

    for load in loads[:3]:
        load.wait()

    column = pl.multiple_of((me // 4) * 128, 128)
    wide = jnp.transpose(jnp.broadcast_to(skip[:, pl.ds(column, 128)], (128, 128)))
    unmixed[pl.ds(0, 128), pl.ds(0, 128)] = wide
    mine = unmixed[pl.ds(pl.multiple_of(lax.rem(me, 4) * OWN, OWN), OWN), pl.ds(0, 128)]
    skip_own[:, pl.ds(0, 128)] = mine
    skip_own[:, pl.ds(128, 128)] = mine

    proj_load.wait()

    @pl.when(me == 0)
    def _():
        proj_local[:, pl.ds(0, HALO), :] = jnp.zeros((3, HALO, WIDTH), BF16)

    @pl.when(me > 0)
    def _():
        halo.wait_recv()

    @pl.loop(0, WIDTH // 128)
    def _(block):
        columns = pl.ds(pl.multiple_of(block * 128, 128), 128)

        @pl.loop(0, ROWS // 128)
        def _(tile):
            start = pl.multiple_of(tile * 128, 128)
            shorts = []
            for feature in range(3):
                taken = proj_local[feature, pl.ds(start, 128 + HALO), columns].astype(F32)
                total = jnp.zeros((128, 128), F32)
                for tap in range(TAPS):
                    total = (
                        total
                        + weight[feature, pl.ds(tap, 1), columns] * taken[HALO - tap : HALO - tap + 128]
                    )
                shorts.append(total)
            places = pl.ds(start, 128)
            gate_send[pl.ds(block * 4, 4), :, places] = (
                jnp.transpose(shorts[0]).astype(BF16).reshape(4, OWN, 128)
            )
            gated_send[pl.ds(block * 4, 4), :, places] = (
                jnp.transpose(shorts[1] * shorts[2]).astype(BF16).reshape(4, OWN, 128)
            )

    gated_got[me] = gated_send[me]
    gate_got[me] = gate_send[me]
    for group in range(GROUPS):
        chans = pl.ds(group * GROUP, GROUP)
        send_all(gated_send.at[:, chans, :], gated_got.at[:, chans, :], GATED + group)
        send_all(gate_send.at[:, chans, :], gate_got.at[:, chans, :], GATE + group)

    for load in loads[3:]:
        load.wait()
    wait_all(spec_got, got_sem.at[SPECTRUM])

    def turned(real, imag, cosine, sine, lanes, sign):
        real, imag = rows_of(real), rows_of(imag)
        c = cosine[:, :, lanes].reshape(SHARDS, 1, 8, 256)
        s = sine[:, :, lanes].reshape(SHARDS, 1, 8, 256)
        if sign > 0:
            new = (c * real - s * imag, c * imag + s * real)
        else:
            new = (c * real + s * imag, c * imag - s * real)
        return tuple(v.reshape(ROWS, 256).astype(BF16) for v in new)

    halves = (pl.ds(0, 256), pl.ds(256, 256))
    uppers = (pl.ds(512, 256), pl.ds(768, 256))
    top, bottom = pl.ds(0, ROWS), pl.ds(ROWS, ROWS)

    @pl.loop(0, GROUPS)
    def _(group):
        chans = pl.ds(pl.multiple_of(group * GROUP, GROUP), GROUP)
        taken = spec_got[:, chans, :].reshape(ROWS, ROWS)
        for low, high in zip(halves, uppers):
            real, imag = dot(taken, spectrum_in[:, low]), dot(taken, spectrum_in[:, high])
            real, imag = turned(real, imag, filter_cos, filter_sin, low, 1)
            stacked_rows[top, low] = real
            stacked_rows[bottom, low] = imag
        for low, high in zip(halves, uppers):
            both = dot(filter_outer[...], stacked_rows[:, low])
            real, imag = turned(both[:ROWS], both[ROWS:], value_cos, value_sin, low, 1)
            stacked_lanes[:, low] = real
            stacked_lanes[:, high] = imag
        for lanes in (*halves, *uppers):
            filter_freq[group, :, lanes] = dot(stacked_lanes[...], forward[:, lanes])

    part_send[...] = jnp.zeros(part_send.shape, F32)

    @pl.loop(0, GROUPS)
    def _(group):
        chans = pl.ds(pl.multiple_of(group * GROUP, GROUP), GROUP)
        wait_all(gated_got.at[:, chans, :], got_sem.at[GATED + group])
        for low, high in zip(halves, uppers):
            both = dot(outer_in[...], gated_got[:, chans, low].reshape(ROWS, 256))
            real, imag = turned(both[:ROWS], both[ROWS:], value_cos, value_sin, low, 1)
            stacked_lanes[:, low] = real
            stacked_lanes[:, high] = imag
        for low, high in zip(halves, uppers):
            real, imag = dot(stacked_lanes[...], forward[:, low]), dot(stacked_lanes[...], forward[:, high])
            f_real, f_imag = filter_freq[group, :, low], filter_freq[group, :, high]
            stacked_rows[top, low] = (f_real * real - f_imag * imag).astype(BF16)
            stacked_rows[bottom, low] = (f_real * imag + f_imag * real).astype(BF16)
        for low, high in zip(halves, uppers):
            real = dot(stacked_rows[top, :], inverse[top, low]) + dot(
                stacked_rows[bottom, :], inverse[bottom, low]
            )
            imag = dot(stacked_rows[top, :], inverse[top, high]) + dot(
                stacked_rows[bottom, :], inverse[bottom, high]
            )
            real, imag = turned(real, imag, value_cos, value_sin, low, -1)
            stacked_lanes[:, low] = real
            stacked_lanes[:, high] = imag
        for low, high in zip(halves, uppers):
            value = dot(outer_out[:, top], stacked_lanes[:, low]) + dot(
                outer_out[:, bottom], stacked_lanes[:, high]
            )
            own = gated_got[:, chans, low].astype(F32)
            unmixed[:, low] = (
                value.reshape(SHARDS, GROUP, 256) + skip_own[chans, :][None] * own
            ).reshape(ROWS, 256)

        wait_all(gate_got.at[:, chans, :], got_sem.at[GATE + group])
        for side in range(2):
            for half, lanes in enumerate(halves):
                value = unmixed[pl.ds(side * 256, 256), lanes].reshape(16, GROUP, 256)
                value = (gate_got[pl.ds(side * 16, 16), chans, lanes].astype(F32) * value).astype(BF16)
                squares = value.astype(F32)
                squares = (squares * squares).reshape(16, 2, 8, 256)
                squares = jnp.sum(jnp.sum(squares, axis=1), axis=1, keepdims=True)
                for index in range(16):
                    device = 2 * index + half if side == 0 else 31 - 2 * index - half
                    mixed_send[side, device, chans, :] = value[index]
                    part_send[device, :, pl.ds(side * 256, 256)] += squares[index]

        @pl.when(group == GROUPS - 1)
        def _():
            send_all(part_send, part_got, POWER)

        for side in range(2):
            mixed_got[side, me, chans, :] = mixed_send[side, me, chans, :]
            send_all(
                mixed_send.at[side, :, chans, :],
                mixed_got.at[side, :, chans, :],
                MIXED + 2 * group + side,
            )

    stores = [
        pltpu.make_async_copy(
            out.at[pl.ds(side * 256, 256), :], h_out.at[pl.ds(side * 256, 256), :], load_sem.at[side]
        )
        for side in range(2)
    ]
    part_got[me] = part_send[me]
    wait_all(part_got, got_sem.at[POWER])
    power = jnp.sum(part_got[...], axis=0)
    power_send[...] = power
    power_got[my_chan] = power

    @pl.loop(1, CHANS)
    def _(k):
        pltpu.make_async_remote_copy(
            src_ref=power_send,
            dst_ref=power_got.at[my_chan],
            send_sem=power_sem.at[0],
            recv_sem=power_sem.at[1],
            device_id={"chan": lax.rem(my_chan + k, CHANS)},
            device_id_type=MESH,
        ).start()

    others = power_got.at[pl.ds(0, CHANS - 1)]
    pltpu.make_async_copy(others, others, power_sem.at[1]).wait()
    scale = lax.rsqrt(jnp.sum(power_got[...], axis=0) * (1.0 / D) + EPSILON)
    scales[...] = jnp.transpose(jnp.broadcast_to(scale, (128, ROWS)))

    for side in range(2):
        rows = pl.ds(side * 256, 256)
        for group in range(GROUPS):
            wait_all(
                mixed_got.at[side, :, pl.ds(group * GROUP, GROUP), :],
                got_sem.at[MIXED + 2 * group + side],
            )

        @pl.loop(0, WIDTH // 128)
        def _(block):
            value = mixed_got[side, pl.ds(block * 4, 4), :, :].reshape(128, 256).astype(F32)
            columns = pl.ds(pl.multiple_of(block * 128, 128), 128)
            out[rows, columns] = (jnp.transpose(value) * scales[rows, :] * gain[:, columns]).astype(BF16)

        stores[side].start()

    for store in stores:
        store.wait()

    @pl.when(me < SHARDS - 1)
    def _():
        halo.wait_send()

    wait_all(spec_send, send_sem.at[SPECTRUM])
    for group in range(GROUPS):
        chans = pl.ds(group * GROUP, GROUP)
        wait_all(gated_send.at[:, chans, :], send_sem.at[GATED + group])
        wait_all(gate_send.at[:, chans, :], send_sem.at[GATE + group])
        for side in range(2):
            wait_all(mixed_send.at[side, :, chans, :], send_sem.at[MIXED + 2 * group + side])
    wait_all(part_send, send_sem.at[POWER])
    pltpu.make_async_copy(others, others, power_sem.at[0]).wait()


def body(proj, short_weight, spectrum, skip, gain):
    constants = tables()
    held = [pltpu.VMEM(c.shape, c.dtype) for c in constants]
    whole = (SHARDS, OWN, ROWS)
    anywhere = pl.BlockSpec(memory_space=pl.ANY)
    value = pl.pallas_call(
        kernel,
        out_shape=jax.ShapeDtypeStruct((ROWS, WIDTH), BF16),
        in_specs=[anywhere] * (5 + len(constants)),
        out_specs=anywhere,
        scratch_shapes=[
            pltpu.VMEM((3, TAPS, WIDTH), F32),
            pltpu.VMEM((1, WIDTH), F32),
            pltpu.VMEM((1, WIDTH), F32),
            pltpu.VMEM((ROWS, WIDTH), BF16),
            pltpu.VMEM((2, 256, WIDTH), BF16),
            pltpu.VMEM((3, HALO + ROWS, WIDTH), BF16),
            pltpu.VMEM(whole, BF16),
            pltpu.VMEM(whole, BF16),
            pltpu.VMEM(whole, BF16),
            pltpu.VMEM(whole, BF16),
            pltpu.VMEM(whole, BF16),
            pltpu.VMEM(whole, BF16),
            pltpu.VMEM((2, SHARDS, OWN, 256), BF16),
            pltpu.VMEM((2, SHARDS, OWN, 256), BF16),
            *held,
            pltpu.VMEM((GROUPS, ROWS, 2 * ROWS), F32),
            pltpu.VMEM((2 * ROWS, ROWS), BF16),
            pltpu.VMEM((ROWS, 2 * ROWS), BF16),
            pltpu.VMEM((ROWS, ROWS), F32),
            pltpu.VMEM((OWN, 256), F32),
            pltpu.VMEM((SHARDS, 1, ROWS), F32),
            pltpu.VMEM((SHARDS, 1, ROWS), F32),
            pltpu.VMEM((1, ROWS), F32),
            pltpu.VMEM((CHANS, 1, ROWS), F32),
            pltpu.VMEM((ROWS, 128), F32),
            pltpu.SemaphoreType.DMA((2,)),
            pltpu.SemaphoreType.DMA((3 + len(constants),)),
            pltpu.SemaphoreType.DMA((2,)),
            pltpu.SemaphoreType.DMA((EXCHANGES,)),
            pltpu.SemaphoreType.DMA((EXCHANGES,)),
            pltpu.SemaphoreType.DMA((2,)),
        ],
        compiler_params=pltpu.CompilerParams(
            collective_id=0, has_side_effects=True, vmem_limit_bytes=56 * 2**20
        ),
    )(proj, spectrum, short_weight, skip[None], gain[None], *(jnp.asarray(c) for c in constants))
    return value.reshape(1, 2, ROWS // 2, WIDTH)


def solution(mesh):
    placed = (
        P(None, "seq", "chan"),
        P(None, None, "chan"),
        P(None, "seq", None, "chan"),
        P("chan"),
        P("chan"),
    )
    return jax.shard_map(
        body, mesh=mesh, in_specs=placed, out_specs=P("seq", None, None, "chan"), check_vma=False
    )
```

```python
import functools
import math

import jax
import jax.numpy as jnp
import ml_dtypes
import numpy as np
from jax import lax
from jax.experimental import pallas as pl
from jax.experimental.pallas import tpu as pltpu
from jax.sharding import PartitionSpec as P

MESH = pl.DeviceIdType.MESH
F32 = jnp.float32
BF16 = jnp.bfloat16

D = 8192
EPSILON = 1e-05
LENGTH = 16384
SHARDS = 32
CHANS = 8
ROWS = 512
WIDTH = 1024
OWN = 32
GROUP = 16
GROUPS = OWN // GROUP
HALO = 16
FINISH = 512
TAPS = 7
SPECTRUM, GATED, GATE, MIXED, POWER, EXCHANGES = 0, 1, 3, 5, 7, 8


def turn(numerator, period):
    angle = np.asarray(numerator % period, np.float64) * (2.0 * math.pi / period)
    return np.cos(angle), np.sin(angle)


@functools.cache
def tables():
    outer = np.arange(SHARDS)
    inner = np.arange(ROWS)
    eye = np.eye(GROUP)
    cos_k, sin_k = turn(np.outer(np.arange(256), inner), ROWS)
    spectrum_in = np.block([[cos_k, sin_k], [-sin_k, cos_k]])
    cos_f, sin_f = turn(np.outer(inner, inner), ROWS)
    forward = np.block([[cos_f, -sin_f], [sin_f, cos_f]])
    inverse = np.block([[cos_f, sin_f], [-sin_f, cos_f]])
    cos_s, sin_s = turn(np.outer(2 * outer + 1, outer), 64)
    cos_a, sin_a = turn(np.outer(4 * outer + 1, outer), 128)
    scale = 2.0 / LENGTH
    filter_outer = scale * np.block(
        [[cos_a @ cos_s.T, -cos_a @ sin_s.T], [-sin_a @ cos_s.T, sin_a @ sin_s.T]]
    )
    outer_in = np.concatenate([cos_a, -sin_a], axis=0)
    outer_out = np.concatenate([cos_a.T, -sin_a.T], axis=1) / LENGTH
    filter_turn = turn(np.outer(2 * outer + 1, inner), 2 * LENGTH)
    value_turn = turn(np.outer(4 * outer + 1, inner), 4 * LENGTH)
    value_turn = (value_turn[0], -value_turn[1])
    matrices = (
        spectrum_in,
        np.kron(filter_outer, eye),
        forward,
        np.kron(outer_in, eye),
        inverse,
        np.kron(outer_out, eye),
    )
    turns = [np.broadcast_to(t[:, None, :], (SHARDS, 8, ROWS)) for t in (*filter_turn, *value_turn)]
    return tuple(m.astype(ml_dtypes.bfloat16) for m in matrices) + tuple(
        np.ascontiguousarray(t, np.float32) for t in turns
    )


def dot(left, right):
    return jnp.dot(left, right, preferred_element_type=F32)


def rows_of(value):
    return value.reshape(SHARDS, 2, 8, value.shape[-1])


def kernel(
    proj,
    spectrum,
    h_weight,
    h_skip,
    h_spectrum_in,
    h_filter_outer,
    h_forward,
    h_outer_in,
    h_inverse,
    h_outer_out,
    h_filter_cos,
    h_filter_sin,
    h_value_cos,
    h_value_sin,
    mixed_got,
    h_scales,
    weight,
    skip,
    spec_local,
    proj_local,
    spec_send,
    gated_send,
    gate_send,
    spec_got,
    gated_got,
    gate_got,
    mixed_send,
    spectrum_in,
    filter_outer,
    forward,
    outer_in,
    inverse,
    outer_out,
    filter_cos,
    filter_sin,
    value_cos,
    value_sin,
    filter_freq,
    stacked_rows,
    stacked_lanes,
    unmixed,
    skip_own,
    part_send,
    part_got,
    power_send,
    power_got,
    scales,
    load_sem,
    table_sem,
    halo_sem,
    send_sem,
    got_sem,
    power_sem,
    own_sem,
):
    me = lax.axis_index("seq")
    my_chan = lax.axis_index("chan")

    spec_load = pltpu.make_async_copy(spectrum.at[:, 1, pl.ds(0, 256), :], spec_local, load_sem.at[0])
    proj_load = pltpu.make_async_copy(proj, proj_local.at[:, pl.ds(HALO, ROWS), :], load_sem.at[1])
    spec_load.start()
    barrier = pltpu.get_barrier_semaphore()

    @pl.loop(1, SHARDS)
    def _(k):
        pl.semaphore_signal(
            barrier, inc=1, device_id={"seq": lax.rem(me + k, SHARDS)}, device_id_type=MESH
        )

    @pl.loop(1, CHANS)
    def _(k):
        pl.semaphore_signal(
            barrier, inc=1, device_id={"chan": lax.rem(my_chan + k, CHANS)}, device_id_type=MESH
        )

    pl.semaphore_wait(barrier, SHARDS - 1 + CHANS - 1)

    halo = pltpu.make_async_remote_copy(
        src_ref=proj.at[:, pl.ds(ROWS - HALO, HALO), :],
        dst_ref=proj_local.at[:, pl.ds(0, HALO), :],
        send_sem=halo_sem.at[0],
        recv_sem=halo_sem.at[1],
        device_id={"seq": lax.rem(me + 1, SHARDS)},
        device_id_type=MESH,
    )

    @pl.when(me < SHARDS - 1)
    def _():
        halo.start()

    def send_one(source, target, device, which):
        pltpu.make_async_remote_copy(
            src_ref=source.at[device],
            dst_ref=target.at[me],
            send_sem=send_sem.at[which],
            recv_sem=got_sem.at[which],
            device_id={"seq": device},
            device_id_type=MESH,
        ).start()

    def send_all(source, target, which):
        @pl.loop(1, SHARDS)
        def _(k):
            send_one(source, target, lax.rem(me + k, SHARDS), which)

    def wait_all(ref, sem):
        part = ref.at[pl.ds(0, SHARDS - 1)]
        pltpu.make_async_copy(part, part, sem).wait()

    spec_load.wait()
    proj_load.start()
    loads = [
        pltpu.make_async_copy(source, target, table_sem.at[index])
        for index, (source, target) in enumerate(
            (
                (h_weight, weight),
                (h_skip, skip),
                (h_spectrum_in, spectrum_in),
                (h_filter_outer, filter_outer),
                (h_forward, forward),
                (h_outer_in, outer_in),
                (h_inverse, inverse),
                (h_outer_out, outer_out),
                (h_filter_cos, filter_cos),
                (h_filter_sin, filter_sin),
                (h_value_cos, value_cos),
                (h_value_sin, value_sin),
            )
        )
    ]
    for load in loads:
        load.start()

    @pl.loop(0, WIDTH // 128)
    def _(step):
        block = lax.rem(me // 4 + step, WIDTH // 128)
        columns = pl.ds(pl.multiple_of(block * 128, 128), 128)
        for part in range(2):
            value = jnp.transpose(spec_local[part, :, columns].astype(F32)).astype(BF16)
            spec_send[pl.ds(block * 4, 4), :, pl.ds(part * 256, 256)] = value.reshape(4, OWN, 256)

        @pl.loop(0, 4)
        def _(k):
            device = block * 4 + lax.rem(me + k, 4)

            @pl.when(device != me)
            def _():
                send_one(spec_send, spec_got, device, SPECTRUM)

    spec_got[me] = spec_send[me]

    for load in loads[:2]:
        load.wait()

    column = pl.multiple_of((me // 4) * 128, 128)
    wide = jnp.transpose(jnp.broadcast_to(skip[:, pl.ds(column, 128)], (128, 128)))
    unmixed[pl.ds(0, 128), pl.ds(0, 128)] = wide
    mine = unmixed[pl.ds(pl.multiple_of(lax.rem(me, 4) * OWN, OWN), OWN), pl.ds(0, 128)]
    skip_own[:, pl.ds(0, 128)] = mine
    skip_own[:, pl.ds(128, 128)] = mine

    proj_load.wait()

    @pl.when(me == 0)
    def _():
        proj_local[:, pl.ds(0, HALO), :] = jnp.zeros((3, HALO, WIDTH), BF16)

    @pl.when(me > 0)
    def _():
        halo.wait_recv()

    @pl.loop(0, WIDTH // 128)
    def _(block):
        columns = pl.ds(pl.multiple_of(block * 128, 128), 128)

        @pl.loop(0, ROWS // 128)
        def _(tile):
            start = pl.multiple_of(tile * 128, 128)
            shorts = []
            for feature in range(3):
                taken = proj_local[feature, pl.ds(start, 128 + HALO), columns].astype(F32)
                total = jnp.zeros((128, 128), F32)
                for tap in range(TAPS):
                    total = (
                        total
                        + weight[feature, pl.ds(tap, 1), columns] * taken[HALO - tap : HALO - tap + 128]
                    )
                shorts.append(total)
            places = pl.ds(start, 128)
            gate_send[pl.ds(block * 4, 4), :, places] = (
                jnp.transpose(shorts[0]).astype(BF16).reshape(4, OWN, 128)
            )
            gated_send[pl.ds(block * 4, 4), :, places] = (
                jnp.transpose(shorts[1] * shorts[2]).astype(BF16).reshape(4, OWN, 128)
            )

    gated_got[me] = gated_send[me]
    gate_got[me] = gate_send[me]
    for group in range(GROUPS):
        chans = pl.ds(group * GROUP, GROUP)
        send_all(gated_send.at[:, chans, :], gated_got.at[:, chans, :], GATED + group)
        send_all(gate_send.at[:, chans, :], gate_got.at[:, chans, :], GATE + group)

    for load in loads[2:]:
        load.wait()
    wait_all(spec_got, got_sem.at[SPECTRUM])

    def turned(real, imag, cosine, sine, lanes, sign):
        real, imag = rows_of(real), rows_of(imag)
        c = cosine[:, :, lanes].reshape(SHARDS, 1, 8, 256)
        s = sine[:, :, lanes].reshape(SHARDS, 1, 8, 256)
        if sign > 0:
            new = (c * real - s * imag, c * imag + s * real)
        else:
            new = (c * real + s * imag, c * imag - s * real)
        return tuple(v.reshape(ROWS, 256).astype(BF16) for v in new)

    halves = (pl.ds(0, 256), pl.ds(256, 256))
    uppers = (pl.ds(512, 256), pl.ds(768, 256))
    top, bottom = pl.ds(0, ROWS), pl.ds(ROWS, ROWS)

    @pl.loop(0, GROUPS)
    def _(group):
        chans = pl.ds(pl.multiple_of(group * GROUP, GROUP), GROUP)
        taken = spec_got[:, chans, :].reshape(ROWS, ROWS)
        for low, high in zip(halves, uppers):
            real, imag = dot(taken, spectrum_in[:, low]), dot(taken, spectrum_in[:, high])
            real, imag = turned(real, imag, filter_cos, filter_sin, low, 1)
            stacked_rows[top, low] = real
            stacked_rows[bottom, low] = imag
        for low, high in zip(halves, uppers):
            both = dot(filter_outer[...], stacked_rows[:, low])
            real, imag = turned(both[:ROWS], both[ROWS:], value_cos, value_sin, low, 1)
            stacked_lanes[:, low] = real
            stacked_lanes[:, high] = imag
        for lanes in (*halves, *uppers):
            filter_freq[group, :, lanes] = dot(stacked_lanes[...], forward[:, lanes])

    def own_store(group):
        chans = pl.ds(pl.multiple_of(group * GROUP, GROUP), GROUP)
        return pltpu.make_async_copy(
            mixed_send.at[me, chans, :], mixed_got.at[me, chans, :], own_sem.at[group]
        )

    part_send[...] = jnp.zeros(part_send.shape, F32)

    @pl.loop(0, GROUPS)
    def _(group):
        chans = pl.ds(pl.multiple_of(group * GROUP, GROUP), GROUP)
        wait_all(gated_got.at[:, chans, :], got_sem.at[GATED + group])
        for low, high in zip(halves, uppers):
            both = dot(outer_in[...], gated_got[:, chans, low].reshape(ROWS, 256))
            real, imag = turned(both[:ROWS], both[ROWS:], value_cos, value_sin, low, 1)
            stacked_lanes[:, low] = real
            stacked_lanes[:, high] = imag
        for low, high in zip(halves, uppers):
            real, imag = dot(stacked_lanes[...], forward[:, low]), dot(stacked_lanes[...], forward[:, high])
            f_real, f_imag = filter_freq[group, :, low], filter_freq[group, :, high]
            stacked_rows[top, low] = (f_real * real - f_imag * imag).astype(BF16)
            stacked_rows[bottom, low] = (f_real * imag + f_imag * real).astype(BF16)
        for low, high in zip(halves, uppers):
            real = dot(stacked_rows[top, :], inverse[top, low]) + dot(
                stacked_rows[bottom, :], inverse[bottom, low]
            )
            imag = dot(stacked_rows[top, :], inverse[top, high]) + dot(
                stacked_rows[bottom, :], inverse[bottom, high]
            )
            real, imag = turned(real, imag, value_cos, value_sin, low, -1)
            stacked_lanes[:, low] = real
            stacked_lanes[:, high] = imag
        for low, high in zip(halves, uppers):
            value = dot(outer_out[:, top], stacked_lanes[:, low]) + dot(
                outer_out[:, bottom], stacked_lanes[:, high]
            )
            own = gated_got[:, chans, low].astype(F32)
            unmixed[:, low] = (
                value.reshape(SHARDS, GROUP, 256) + skip_own[chans, :][None] * own
            ).reshape(ROWS, 256)

        wait_all(gate_got.at[:, chans, :], got_sem.at[GATE + group])
        for side in range(2):
            for half, lanes in enumerate(halves):
                value = unmixed[pl.ds(side * 256, 256), lanes].reshape(16, GROUP, 256)
                value = (gate_got[pl.ds(side * 16, 16), chans, lanes].astype(F32) * value).astype(BF16)
                squares = value.astype(F32)
                squares = (squares * squares).reshape(16, 2, 8, 256)
                squares = jnp.sum(jnp.sum(squares, axis=1), axis=1, keepdims=True)
                for index in range(16):
                    device = 2 * index + half if side == 0 else 31 - 2 * index - half
                    mixed_send[device, chans, pl.ds(side * 256, 256)] = value[index]
                    part_send[device, :, pl.ds(side * 256, 256)] += squares[index]

        @pl.when(group == GROUPS - 1)
        def _():
            send_all(part_send, part_got, POWER)

        own_store(group).start()
        send_all(mixed_send.at[:, chans, :], mixed_got.at[:, chans, :], MIXED + group)

    part_got[me] = part_send[me]
    wait_all(part_got, got_sem.at[POWER])
    power = jnp.sum(part_got[...], axis=0)
    power_send[...] = power
    power_got[my_chan] = power

    @pl.loop(1, CHANS)
    def _(k):
        pltpu.make_async_remote_copy(
            src_ref=power_send,
            dst_ref=power_got.at[my_chan],
            send_sem=power_sem.at[0],
            recv_sem=power_sem.at[1],
            device_id={"chan": lax.rem(my_chan + k, CHANS)},
            device_id_type=MESH,
        ).start()

    others = power_got.at[pl.ds(0, CHANS - 1)]
    pltpu.make_async_copy(others, others, power_sem.at[1]).wait()
    scales[...] = lax.rsqrt(jnp.sum(power_got[...], axis=0) * (1.0 / D) + EPSILON)

    store = pltpu.make_async_copy(scales, h_scales, load_sem.at[0])
    store.start()
    for group in range(GROUPS):
        wait_all(mixed_got.at[:, pl.ds(group * GROUP, GROUP), :], got_sem.at[MIXED + group])
        own_store(group).wait()
    store.wait()

    @pl.when(me < SHARDS - 1)
    def _():
        halo.wait_send()

    wait_all(spec_send, send_sem.at[SPECTRUM])
    for group in range(GROUPS):
        chans = pl.ds(group * GROUP, GROUP)
        wait_all(gated_send.at[:, chans, :], send_sem.at[GATED + group])
        wait_all(gate_send.at[:, chans, :], send_sem.at[GATE + group])
        wait_all(mixed_send.at[:, chans, :], send_sem.at[MIXED + group])
    wait_all(part_send, send_sem.at[POWER])
    pltpu.make_async_copy(others, others, power_sem.at[0]).wait()


def finish(h_mixed, h_scales, h_gain, h_out, mixed, scales, gain, out, load_sem, store_sem):
    steps = WIDTH // FINISH
    loads, stores = [], []
    for step in range(steps):
        owners = pl.ds(step * FINISH // OWN, FINISH // OWN)
        columns = pl.ds(step * FINISH, FINISH)
        loads.append(pltpu.make_async_copy(h_mixed.at[owners], mixed.at[owners], load_sem.at[step]))
        stores.append(pltpu.make_async_copy(out.at[:, columns], h_out.at[:, columns], store_sem.at[step]))
    small = [
        pltpu.make_async_copy(h_scales, scales, load_sem.at[steps]),
        pltpu.make_async_copy(h_gain, gain, load_sem.at[steps + 1]),
    ]
    for load in small + loads:
        load.start()
    for load in small:
        load.wait()
    for step in range(steps):
        loads[step].wait()
        for block in range(step * FINISH // 128, (step + 1) * FINISH // 128):
            columns = pl.ds(block * 128, 128)
            value = mixed[pl.ds(block * 4, 4), :, :].reshape(128, ROWS).astype(F32)
            value = jnp.transpose(value * scales[...])
            out[:, columns] = (value * gain[:, columns]).astype(BF16)
        stores[step].start()
    for store in stores:
        store.wait()


def body(proj, short_weight, spectrum, skip, gain):
    constants = tables()
    held = [pltpu.VMEM(c.shape, c.dtype) for c in constants]
    whole = (SHARDS, OWN, ROWS)
    anywhere = pl.BlockSpec(memory_space=pl.ANY)
    mixed, scales = pl.pallas_call(
        kernel,
        out_shape=(
            jax.ShapeDtypeStruct(whole, BF16),
            jax.ShapeDtypeStruct((1, ROWS), F32),
        ),
        in_specs=[anywhere] * (4 + len(constants)),
        out_specs=(anywhere, anywhere),
        scratch_shapes=[
            pltpu.VMEM((3, TAPS, WIDTH), F32),
            pltpu.VMEM((1, WIDTH), F32),
            pltpu.VMEM((2, 256, WIDTH), BF16),
            pltpu.VMEM((3, HALO + ROWS, WIDTH), BF16),
            pltpu.VMEM(whole, BF16),
            pltpu.VMEM(whole, BF16),
            pltpu.VMEM(whole, BF16),
            pltpu.VMEM(whole, BF16),
            pltpu.VMEM(whole, BF16),
            pltpu.VMEM(whole, BF16),
            pltpu.VMEM(whole, BF16),
            *held,
            pltpu.VMEM((GROUPS, ROWS, 2 * ROWS), F32),
            pltpu.VMEM((2 * ROWS, ROWS), BF16),
            pltpu.VMEM((ROWS, 2 * ROWS), BF16),
            pltpu.VMEM((ROWS, ROWS), F32),
            pltpu.VMEM((OWN, 256), F32),
            pltpu.VMEM((SHARDS, 1, ROWS), F32),
            pltpu.VMEM((SHARDS, 1, ROWS), F32),
            pltpu.VMEM((1, ROWS), F32),
            pltpu.VMEM((CHANS, 1, ROWS), F32),
            pltpu.VMEM((1, ROWS), F32),
            pltpu.SemaphoreType.DMA((2,)),
            pltpu.SemaphoreType.DMA((2 + len(constants),)),
            pltpu.SemaphoreType.DMA((2,)),
            pltpu.SemaphoreType.DMA((EXCHANGES,)),
            pltpu.SemaphoreType.DMA((EXCHANGES,)),
            pltpu.SemaphoreType.DMA((2,)),
            pltpu.SemaphoreType.DMA((GROUPS,)),
        ],
        compiler_params=pltpu.CompilerParams(
            collective_id=0, has_side_effects=True, vmem_limit_bytes=56 * 2**20
        ),
    )(proj, spectrum, short_weight, skip[None], *(jnp.asarray(c) for c in constants))
    value = pl.pallas_call(
        finish,
        out_shape=jax.ShapeDtypeStruct((ROWS, WIDTH), BF16),
        in_specs=[anywhere] * 3,
        out_specs=anywhere,
        scratch_shapes=[
            pltpu.VMEM(whole, BF16),
            pltpu.VMEM((1, ROWS), F32),
            pltpu.VMEM((1, WIDTH), F32),
            pltpu.VMEM((ROWS, WIDTH), BF16),
            pltpu.SemaphoreType.DMA((WIDTH // FINISH + 2,)),
            pltpu.SemaphoreType.DMA((WIDTH // FINISH,)),
        ],
    )(mixed, scales, gain[None])
    return value.reshape(1, 2, ROWS // 2, WIDTH)


def solution(mesh):
    placed = (
        P(None, "seq", "chan"),
        P(None, None, "chan"),
        P(None, "seq", None, "chan"),
        P("chan"),
        P("chan"),
    )
    return jax.shard_map(
        body, mesh=mesh, in_specs=placed, out_specs=P("seq", None, None, "chan"), check_vma=False
    )
```

```python
import functools
import math

import jax
import jax.numpy as jnp
import ml_dtypes
import numpy as np
from jax import lax
from jax.experimental import pallas as pl
from jax.experimental.pallas import tpu as pltpu
from jax.sharding import PartitionSpec as P

MESH = pl.DeviceIdType.MESH
F32 = jnp.float32
BF16 = jnp.bfloat16

D = 8192
EPSILON = 1e-05
LENGTH = 16384
SHARDS = 32
CHANS = 8
ROWS = 512
WIDTH = 1024
OWN = 32
GROUP = 16
GROUPS = OWN // GROUP
HALO = 16
FINISH = 256
TAPS = 7
SPECTRUM, GATED, GATE, MIXED, POWER, EXCHANGES = 0, 1, 3, 5, 7, 8


def turn(numerator, period):
    angle = np.asarray(numerator % period, np.float64) * (2.0 * math.pi / period)
    return np.cos(angle), np.sin(angle)


@functools.cache
def tables():
    outer = np.arange(SHARDS)
    inner = np.arange(ROWS)
    eye = np.eye(GROUP)
    cos_k, sin_k = turn(np.outer(np.arange(256), inner), ROWS)
    spectrum_in = np.block([[cos_k, sin_k], [-sin_k, cos_k]])
    cos_f, sin_f = turn(np.outer(inner, inner), ROWS)
    forward = np.block([[cos_f, -sin_f], [sin_f, cos_f]])
    inverse = np.block([[cos_f, sin_f], [-sin_f, cos_f]])
    cos_s, sin_s = turn(np.outer(2 * outer + 1, outer), 64)
    cos_a, sin_a = turn(np.outer(4 * outer + 1, outer), 128)
    scale = 2.0 / LENGTH
    filter_outer = scale * np.block(
        [[cos_a @ cos_s.T, -cos_a @ sin_s.T], [-sin_a @ cos_s.T, sin_a @ sin_s.T]]
    )
    outer_in = np.concatenate([cos_a, -sin_a], axis=0)
    outer_out = np.concatenate([cos_a.T, -sin_a.T], axis=1) / LENGTH
    filter_turn = turn(np.outer(2 * outer + 1, inner), 2 * LENGTH)
    value_turn = turn(np.outer(4 * outer + 1, inner), 4 * LENGTH)
    value_turn = (value_turn[0], -value_turn[1])
    matrices = (
        spectrum_in,
        np.kron(filter_outer, eye),
        forward,
        np.kron(outer_in, eye),
        inverse,
        np.kron(outer_out, eye),
    )
    turns = [np.broadcast_to(t[:, None, :], (SHARDS, 8, ROWS)) for t in (*filter_turn, *value_turn)]
    return tuple(m.astype(ml_dtypes.bfloat16) for m in matrices) + tuple(
        np.ascontiguousarray(t, np.float32) for t in turns
    )


def dot(left, right):
    return jnp.dot(left, right, preferred_element_type=F32)


def rows_of(value):
    return value.reshape(SHARDS, 2, 8, value.shape[-1])


def kernel(
    proj,
    spectrum,
    h_weight,
    h_skip,
    h_spectrum_in,
    h_filter_outer,
    h_forward,
    h_outer_in,
    h_inverse,
    h_outer_out,
    h_filter_cos,
    h_filter_sin,
    h_value_cos,
    h_value_sin,
    mixed_got,
    h_scales,
    weight,
    skip,
    spec_local,
    proj_local,
    spec_send,
    gated_send,
    gate_send,
    spec_got,
    gated_got,
    gate_got,
    mixed_send,
    spectrum_in,
    filter_outer,
    forward,
    outer_in,
    inverse,
    outer_out,
    filter_cos,
    filter_sin,
    value_cos,
    value_sin,
    filter_freq,
    stacked_rows,
    stacked_lanes,
    unmixed,
    skip_own,
    part_send,
    part_got,
    power_send,
    power_got,
    scales,
    load_sem,
    table_sem,
    halo_sem,
    send_sem,
    got_sem,
    power_sem,
    own_sem,
):
    me = lax.axis_index("seq")
    my_chan = lax.axis_index("chan")

    spec_load = pltpu.make_async_copy(spectrum.at[:, 1, pl.ds(0, 256), :], spec_local, load_sem.at[0])
    proj_load = pltpu.make_async_copy(proj, proj_local.at[:, pl.ds(HALO, ROWS), :], load_sem.at[1])
    spec_load.start()
    barrier = pltpu.get_barrier_semaphore()

    @pl.loop(1, SHARDS)
    def _(k):
        pl.semaphore_signal(
            barrier, inc=1, device_id={"seq": lax.rem(me + k, SHARDS)}, device_id_type=MESH
        )

    @pl.loop(1, CHANS)
    def _(k):
        pl.semaphore_signal(
            barrier, inc=1, device_id={"chan": lax.rem(my_chan + k, CHANS)}, device_id_type=MESH
        )

    pl.semaphore_wait(barrier, SHARDS - 1 + CHANS - 1)

    halo = pltpu.make_async_remote_copy(
        src_ref=proj.at[:, pl.ds(ROWS - HALO, HALO), :],
        dst_ref=proj_local.at[:, pl.ds(0, HALO), :],
        send_sem=halo_sem.at[0],
        recv_sem=halo_sem.at[1],
        device_id={"seq": lax.rem(me + 1, SHARDS)},
        device_id_type=MESH,
    )

    @pl.when(me < SHARDS - 1)
    def _():
        halo.start()

    def send_one(source, target, device, which):
        pltpu.make_async_remote_copy(
            src_ref=source.at[device],
            dst_ref=target.at[me],
            send_sem=send_sem.at[which],
            recv_sem=got_sem.at[which],
            device_id={"seq": device},
            device_id_type=MESH,
        ).start()

    def send_all(source, target, which):
        @pl.loop(1, SHARDS)
        def _(k):
            send_one(source, target, lax.rem(me + k, SHARDS), which)

    def wait_all(ref, sem):
        part = ref.at[pl.ds(0, SHARDS - 1)]
        pltpu.make_async_copy(part, part, sem).wait()

    spec_load.wait()
    proj_load.start()
    loads = [
        pltpu.make_async_copy(source, target, table_sem.at[index])
        for index, (source, target) in enumerate(
            (
                (h_weight, weight),
                (h_skip, skip),
                (h_spectrum_in, spectrum_in),
                (h_filter_outer, filter_outer),
                (h_forward, forward),
                (h_outer_in, outer_in),
                (h_inverse, inverse),
                (h_outer_out, outer_out),
                (h_filter_cos, filter_cos),
                (h_filter_sin, filter_sin),
                (h_value_cos, value_cos),
                (h_value_sin, value_sin),
            )
        )
    ]
    for load in loads:
        load.start()

    @pl.loop(0, WIDTH // 128)
    def _(step):
        block = lax.rem(me // 4 + step, WIDTH // 128)
        columns = pl.ds(pl.multiple_of(block * 128, 128), 128)
        for part in range(2):
            value = jnp.transpose(spec_local[part, :, columns].astype(F32)).astype(BF16)
            spec_send[pl.ds(block * 4, 4), :, pl.ds(part * 256, 256)] = value.reshape(4, OWN, 256)

        @pl.loop(0, 4)
        def _(k):
            device = block * 4 + lax.rem(me + k, 4)

            @pl.when(device != me)
            def _():
                send_one(spec_send, spec_got, device, SPECTRUM)

    spec_got[me] = spec_send[me]

    for load in loads[:2]:
        load.wait()

    column = pl.multiple_of((me // 4) * 128, 128)
    wide = jnp.transpose(jnp.broadcast_to(skip[:, pl.ds(column, 128)], (128, 128)))
    unmixed[pl.ds(0, 128), pl.ds(0, 128)] = wide
    mine = unmixed[pl.ds(pl.multiple_of(lax.rem(me, 4) * OWN, OWN), OWN), pl.ds(0, 128)]
    skip_own[:, pl.ds(0, 128)] = mine
    skip_own[:, pl.ds(128, 128)] = mine

    proj_load.wait()

    @pl.when(me == 0)
    def _():
        proj_local[:, pl.ds(0, HALO), :] = jnp.zeros((3, HALO, WIDTH), BF16)

    @pl.when(me > 0)
    def _():
        halo.wait_recv()

    @pl.loop(0, WIDTH // 128)
    def _(block):
        columns = pl.ds(pl.multiple_of(block * 128, 128), 128)

        @pl.loop(0, ROWS // 128)
        def _(tile):
            start = pl.multiple_of(tile * 128, 128)
            shorts = []
            for feature in range(3):
                taken = proj_local[feature, pl.ds(start, 128 + HALO), columns].astype(F32)
                total = jnp.zeros((128, 128), F32)
                for tap in range(TAPS):
                    total = (
                        total
                        + weight[feature, pl.ds(tap, 1), columns] * taken[HALO - tap : HALO - tap + 128]
                    )
                shorts.append(total)
            places = pl.ds(start, 128)
            gate_send[pl.ds(block * 4, 4), :, places] = (
                jnp.transpose(shorts[0]).astype(BF16).reshape(4, OWN, 128)
            )
            gated_send[pl.ds(block * 4, 4), :, places] = (
                jnp.transpose(shorts[1] * shorts[2]).astype(BF16).reshape(4, OWN, 128)
            )

    gated_got[me] = gated_send[me]
    gate_got[me] = gate_send[me]
    for group in range(GROUPS):
        chans = pl.ds(group * GROUP, GROUP)
        send_all(gated_send.at[:, chans, :], gated_got.at[:, chans, :], GATED + group)
        send_all(gate_send.at[:, chans, :], gate_got.at[:, chans, :], GATE + group)

    for load in loads[2:]:
        load.wait()
    wait_all(spec_got, got_sem.at[SPECTRUM])

    def turned(real, imag, cosine, sine, lanes, sign):
        real, imag = rows_of(real), rows_of(imag)
        c = cosine[:, :, lanes].reshape(SHARDS, 1, 8, 256)
        s = sine[:, :, lanes].reshape(SHARDS, 1, 8, 256)
        if sign > 0:
            new = (c * real - s * imag, c * imag + s * real)
        else:
            new = (c * real + s * imag, c * imag - s * real)
        return tuple(v.reshape(ROWS, 256).astype(BF16) for v in new)

    halves = (pl.ds(0, 256), pl.ds(256, 256))
    uppers = (pl.ds(512, 256), pl.ds(768, 256))
    top, bottom = pl.ds(0, ROWS), pl.ds(ROWS, ROWS)

    @pl.loop(0, GROUPS)
    def _(group):
        chans = pl.ds(pl.multiple_of(group * GROUP, GROUP), GROUP)
        taken = spec_got[:, chans, :].reshape(ROWS, ROWS)
        for low, high in zip(halves, uppers):
            real, imag = dot(taken, spectrum_in[:, low]), dot(taken, spectrum_in[:, high])
            real, imag = turned(real, imag, filter_cos, filter_sin, low, 1)
            stacked_rows[top, low] = real
            stacked_rows[bottom, low] = imag
        for low, high in zip(halves, uppers):
            both = dot(filter_outer[...], stacked_rows[:, low])
            real, imag = turned(both[:ROWS], both[ROWS:], value_cos, value_sin, low, 1)
            stacked_lanes[:, low] = real
            stacked_lanes[:, high] = imag
        for lanes in (*halves, *uppers):
            filter_freq[group, :, lanes] = dot(stacked_lanes[...], forward[:, lanes])

    def own_store(group):
        chans = pl.ds(pl.multiple_of(group * GROUP, GROUP), GROUP)
        return pltpu.make_async_copy(
            mixed_send.at[me, chans, :], mixed_got.at[me, chans, :], own_sem.at[group]
        )

    part_send[...] = jnp.zeros(part_send.shape, F32)

    @pl.loop(0, GROUPS)
    def _(group):
        chans = pl.ds(pl.multiple_of(group * GROUP, GROUP), GROUP)
        wait_all(gated_got.at[:, chans, :], got_sem.at[GATED + group])
        for low, high in zip(halves, uppers):
            both = dot(outer_in[...], gated_got[:, chans, low].reshape(ROWS, 256))
            real, imag = turned(both[:ROWS], both[ROWS:], value_cos, value_sin, low, 1)
            stacked_lanes[:, low] = real
            stacked_lanes[:, high] = imag
        for low, high in zip(halves, uppers):
            real, imag = dot(stacked_lanes[...], forward[:, low]), dot(stacked_lanes[...], forward[:, high])
            f_real, f_imag = filter_freq[group, :, low], filter_freq[group, :, high]
            stacked_rows[top, low] = (f_real * real - f_imag * imag).astype(BF16)
            stacked_rows[bottom, low] = (f_real * imag + f_imag * real).astype(BF16)
        for low, high in zip(halves, uppers):
            real = dot(stacked_rows[top, :], inverse[top, low]) + dot(
                stacked_rows[bottom, :], inverse[bottom, low]
            )
            imag = dot(stacked_rows[top, :], inverse[top, high]) + dot(
                stacked_rows[bottom, :], inverse[bottom, high]
            )
            real, imag = turned(real, imag, value_cos, value_sin, low, -1)
            stacked_lanes[:, low] = real
            stacked_lanes[:, high] = imag
        for low, high in zip(halves, uppers):
            value = dot(outer_out[:, top], stacked_lanes[:, low]) + dot(
                outer_out[:, bottom], stacked_lanes[:, high]
            )
            own = gated_got[:, chans, low].astype(F32)
            unmixed[:, low] = (
                value.reshape(SHARDS, GROUP, 256) + skip_own[chans, :][None] * own
            ).reshape(ROWS, 256)

        wait_all(gate_got.at[:, chans, :], got_sem.at[GATE + group])
        for side in range(2):
            for half, lanes in enumerate(halves):
                value = unmixed[pl.ds(side * 256, 256), lanes].reshape(16, GROUP, 256)
                value = (gate_got[pl.ds(side * 16, 16), chans, lanes].astype(F32) * value).astype(BF16)
                squares = value.astype(F32)
                squares = (squares * squares).reshape(16, 2, 8, 256)
                squares = jnp.sum(jnp.sum(squares, axis=1), axis=1, keepdims=True)
                for index in range(16):
                    device = 2 * index + half if side == 0 else 31 - 2 * index - half
                    mixed_send[device, chans, pl.ds(side * 256, 256)] = value[index]
                    part_send[device, :, pl.ds(side * 256, 256)] += squares[index]

        @pl.when(group == GROUPS - 1)
        def _():
            send_all(part_send, part_got, POWER)

        own_store(group).start()
        send_all(mixed_send.at[:, chans, :], mixed_got.at[:, chans, :], MIXED + group)

    part_got[me] = part_send[me]
    wait_all(part_got, got_sem.at[POWER])
    power = jnp.sum(part_got[...], axis=0)
    power_send[...] = power
    power_got[my_chan] = power

    @pl.loop(1, CHANS)
    def _(k):
        pltpu.make_async_remote_copy(
            src_ref=power_send,
            dst_ref=power_got.at[my_chan],
            send_sem=power_sem.at[0],
            recv_sem=power_sem.at[1],
            device_id={"chan": lax.rem(my_chan + k, CHANS)},
            device_id_type=MESH,
        ).start()

    others = power_got.at[pl.ds(0, CHANS - 1)]
    pltpu.make_async_copy(others, others, power_sem.at[1]).wait()
    scales[...] = lax.rsqrt(jnp.sum(power_got[...], axis=0) * (1.0 / D) + EPSILON)

    store = pltpu.make_async_copy(scales, h_scales, load_sem.at[0])
    store.start()
    for group in range(GROUPS):
        wait_all(mixed_got.at[:, pl.ds(group * GROUP, GROUP), :], got_sem.at[MIXED + group])
        own_store(group).wait()
    store.wait()

    @pl.when(me < SHARDS - 1)
    def _():
        halo.wait_send()

    wait_all(spec_send, send_sem.at[SPECTRUM])
    for group in range(GROUPS):
        chans = pl.ds(group * GROUP, GROUP)
        wait_all(gated_send.at[:, chans, :], send_sem.at[GATED + group])
        wait_all(gate_send.at[:, chans, :], send_sem.at[GATE + group])
        wait_all(mixed_send.at[:, chans, :], send_sem.at[MIXED + group])
    wait_all(part_send, send_sem.at[POWER])
    pltpu.make_async_copy(others, others, power_sem.at[0]).wait()


def finish(h_mixed, h_scales, h_gain, h_out, mixed, scales, gain, out, load_sem, store_sem):
    steps = WIDTH // FINISH
    loads, stores = [], []
    for step in range(steps):
        owners = pl.ds(step * FINISH // OWN, FINISH // OWN)
        columns = pl.ds(step * FINISH, FINISH)
        loads.append(pltpu.make_async_copy(h_mixed.at[owners], mixed.at[owners], load_sem.at[step]))
        stores.append(pltpu.make_async_copy(out.at[:, columns], h_out.at[:, columns], store_sem.at[step]))
    small = [
        pltpu.make_async_copy(h_scales, scales, load_sem.at[steps]),
        pltpu.make_async_copy(h_gain, gain, load_sem.at[steps + 1]),
    ]
    for load in small + loads:
        load.start()
    for load in small:
        load.wait()
    for step in range(steps):
        loads[step].wait()
        for block in range(step * FINISH // 128, (step + 1) * FINISH // 128):
            columns = pl.ds(block * 128, 128)
            value = mixed[pl.ds(block * 4, 4), :, :].reshape(128, ROWS).astype(F32)
            value = jnp.transpose(value * scales[...])
            out[:, columns] = (value * gain[:, columns]).astype(BF16)
        stores[step].start()
    for store in stores:
        store.wait()


def body(proj, short_weight, spectrum, skip, gain):
    constants = tables()
    held = [pltpu.VMEM(c.shape, c.dtype) for c in constants]
    whole = (SHARDS, OWN, ROWS)
    anywhere = pl.BlockSpec(memory_space=pl.ANY)
    mixed, scales = pl.pallas_call(
        kernel,
        out_shape=(
            jax.ShapeDtypeStruct(whole, BF16),
            jax.ShapeDtypeStruct((1, ROWS), F32),
        ),
        in_specs=[anywhere] * (4 + len(constants)),
        out_specs=(anywhere, anywhere),
        scratch_shapes=[
            pltpu.VMEM((3, TAPS, WIDTH), F32),
            pltpu.VMEM((1, WIDTH), F32),
            pltpu.VMEM((2, 256, WIDTH), BF16),
            pltpu.VMEM((3, HALO + ROWS, WIDTH), BF16),
            pltpu.VMEM(whole, BF16),
            pltpu.VMEM(whole, BF16),
            pltpu.VMEM(whole, BF16),
            pltpu.VMEM(whole, BF16),
            pltpu.VMEM(whole, BF16),
            pltpu.VMEM(whole, BF16),
            pltpu.VMEM(whole, BF16),
            *held,
            pltpu.VMEM((GROUPS, ROWS, 2 * ROWS), F32),
            pltpu.VMEM((2 * ROWS, ROWS), BF16),
            pltpu.VMEM((ROWS, 2 * ROWS), BF16),
            pltpu.VMEM((ROWS, ROWS), F32),
            pltpu.VMEM((OWN, 256), F32),
            pltpu.VMEM((SHARDS, 1, ROWS), F32),
            pltpu.VMEM((SHARDS, 1, ROWS), F32),
            pltpu.VMEM((1, ROWS), F32),
            pltpu.VMEM((CHANS, 1, ROWS), F32),
            pltpu.VMEM((1, ROWS), F32),
            pltpu.SemaphoreType.DMA((2,)),
            pltpu.SemaphoreType.DMA((2 + len(constants),)),
            pltpu.SemaphoreType.DMA((2,)),
            pltpu.SemaphoreType.DMA((EXCHANGES,)),
            pltpu.SemaphoreType.DMA((EXCHANGES,)),
            pltpu.SemaphoreType.DMA((2,)),
            pltpu.SemaphoreType.DMA((GROUPS,)),
        ],
        compiler_params=pltpu.CompilerParams(
            collective_id=0, has_side_effects=True, vmem_limit_bytes=56 * 2**20
        ),
    )(proj, spectrum, short_weight, skip[None], *(jnp.asarray(c) for c in constants))
    value = pl.pallas_call(
        finish,
        out_shape=jax.ShapeDtypeStruct((ROWS, WIDTH), BF16),
        in_specs=[anywhere] * 3,
        out_specs=anywhere,
        scratch_shapes=[
            pltpu.VMEM(whole, BF16),
            pltpu.VMEM((1, ROWS), F32),
            pltpu.VMEM((1, WIDTH), F32),
            pltpu.VMEM((ROWS, WIDTH), BF16),
            pltpu.SemaphoreType.DMA((WIDTH // FINISH + 2,)),
            pltpu.SemaphoreType.DMA((WIDTH // FINISH,)),
        ],
    )(mixed, scales, gain[None])
    return value.reshape(1, 2, ROWS // 2, WIDTH)


def solution(mesh):
    placed = (
        P(None, "seq", "chan"),
        P(None, None, "chan"),
        P(None, "seq", None, "chan"),
        P("chan"),
        P("chan"),
    )
    return jax.shard_map(
        body, mesh=mesh, in_specs=placed, out_specs=P("seq", None, None, "chan"), check_vma=False
    )
```
